128 devices in a mesh: blk: 32 (over y, x, z_hi), occ: 4 (over z_lo, core).
Axes of the slice: x: 4, y: 4, z: 4 (z_hi: 2, z_lo: 2; z = z_hi * 2 + z_lo), core: 2. Of those that a mesh axis runs over, the one named last changes fastest.
Arguments:
- amplitudes: bfloat16 [64, 64, 49152], P('occ', None, 'blk'), may hold values from -6 to 6
- integrals: bfloat16 [49152, 4608], P('blk'), may hold values from -0.25 to 0.25
- pair_irrep: int32 [49152], replicated, may hold values from 0 to 7, as said below
- pair_energy: float32 [49152], P('blk'), may hold values from 0.5 to 3
- occ_energy: float32 [64], replicated, may hold values from -1.5 to -0.3
Outputs:
- update: float32 [64, 64, 49152], P('occ', None, 'blk')
The draws below stay inside these ranges and needn't reach their ends.
Inputs may be any that keep to these rules, and one draw needn't show every extreme that they name: `pair_irrep`: labels are constant over aligned runs of 128 pairs and are non-decreasing within each block of 1536 pairs.
All inputs are finite; a program needn't handle non-finite values.
Results may differ from the reference program's by a relative error of at most 0.0003.
Values may be sent and summed in bfloat16 or wider, within the bound.
No kernel may reach another device: no remote copies, remote signals or barrier semaphores. Data moves between devices by JAX's collectives and lax.ppermute only.
A program may use at most 128 MiB of HBM per device.

```python
import jax
import jax.numpy as jnp
from jax import lax

NOCC = 64
PB = 1536
RUN = 128
NBLK = 32
VPAIRS = 49152


def draw_pair_irrep(key, part):
    key = jax.random.fold_in(key, 11)
    runs = PB // RUN
    run_labels = jax.random.randint(key, (NBLK, runs), 0, 8, dtype=jnp.int32)
    run_labels = run_labels.at[0, 0].set(0).at[0, runs - 1].set(7)
    run_labels = jnp.sort(run_labels, axis=1)
    return jnp.repeat(run_labels, RUN, axis=1).reshape(NBLK * PB).astype(jnp.int32)


def block_levels(own_key, extent, pieces, least, high):
    def one(axis_at, parts):
        heights = jax.random.uniform(jax.random.fold_in(jax.random.fold_in(own_key, 6), axis_at), (parts,), jnp.float32, least / len(pieces), high / len(pieces))
        return jnp.repeat(jnp.exp(heights), extent[axis_at] // parts).reshape((-1,) + (1,) * (len(extent) - axis_at - 1))

    loudness = one(*pieces[0])
    for cut in pieces[1:]:
        loudness = loudness * one(*cut)
    return loudness


def noise(key, shape, width, most, cuts=(), kind=jnp.bfloat16):
    result = width * jax.random.normal(key, shape, jnp.float32)
    if cuts:
        result = result * block_levels(key, shape, cuts, -0.22, 0.18)
    return jnp.clip(result, -most, most).astype(kind)


def setup_inputs(seed: int = 0) -> dict:
    splits = jax.random.split(jax.random.key(seed), 6)
    amplitudes = noise(splits[0], (NOCC, NOCC, VPAIRS), 1.0, 6.0, ((0, 4), (2, 32)))
    integrals = noise(splits[1], (VPAIRS, 3 * PB), (3 * PB // 8) ** -0.5, 0.25, ((0, 32),))
    pair_irrep = draw_pair_irrep(jax.random.fold_in(splits[5], 71), 0)
    pair_energy = jnp.clip(0.5 + 2.5 * jax.random.uniform(splits[3], (VPAIRS,), jnp.float32) ** block_levels(splits[3], (VPAIRS,), ((0, 32),), -0.2, 0.2), 0.5, 3.0)
    occ_energy = jnp.clip(jax.random.uniform(splits[4], (NOCC,), jnp.float32, -1.5, -0.3), -1.5, -0.3)
    return {"amplitudes": amplitudes, "integrals": integrals, "pair_irrep": pair_irrep, "pair_energy": pair_energy, "occ_energy": occ_energy}


def reference(amplitudes, integrals, pair_irrep, pair_energy, occ_energy):
    flat = amplitudes.reshape(NOCC * NOCC, NBLK, PB)
    blocks = integrals.reshape(NBLK, PB, 3, PB)
    labels = pair_irrep.reshape(NBLK, PB)

    def one_block(k):
        total = jnp.zeros((NOCC * NOCC, PB), jnp.float32)
        col_labels = lax.dynamic_index_in_dim(labels, k, 0, keepdims=False)
        for s in range(3):
            source = ((k - s) % NBLK).astype(jnp.int32)
            left = lax.dynamic_index_in_dim(flat, source, 1, keepdims=False)
            slab = lax.dynamic_index_in_dim(blocks, source, 0, keepdims=False)[:, s, :]
            row_labels = lax.dynamic_index_in_dim(labels, source, 0, keepdims=False)
            slab = jnp.where(row_labels[:, None] == col_labels[None, :], slab, jnp.zeros((), slab.dtype))
            total = total + jnp.dot(left, slab, preferred_element_type=jnp.float32)
        return total

    ladder = lax.map(one_block, jnp.arange(NBLK, dtype=jnp.int32))
    ladder = ladder.transpose(1, 0, 2).reshape(NOCC, NOCC, NBLK * PB)
    swapped = ladder - ladder.transpose(1, 0, 2)
    denominator = pair_energy[None, None, :] - occ_energy[:, None, None] - occ_energy[None, :, None]
    return swapped / denominator
```

```python
import functools

import jax
import jax.numpy as jnp
from jax import lax
from jax.experimental import pallas as pl
from jax.experimental.pallas import tpu as pltpu
from jax.sharding import PartitionSpec as P

BOTH = ("blk", "occ")
RUN = 128
OCT = 8
G = 128
PAD = 16
LEVELS = 32000.0
STEPS = 256.0
VMEM = 60 * 1024 * 1024


def routes(where):
    pairs = []
    for blk in range(32):
        for occ in range(4):
            to_blk, to_occ = where(blk, occ)
            pairs.append((blk * 4 + occ, (to_blk % 32) * 4 + to_occ))
    return pairs


def send(value, where):
    return lax.ppermute(value, BOTH, routes(where))


def encode(value, out_ref):
    rows = value.shape[0]
    most = jnp.max(jnp.abs(value), axis=0, keepdims=True)
    code = jnp.ceil(jnp.log2(jnp.maximum(most, 2.0**-120)) * STEPS)
    up = jnp.exp2(code * (-1.0 / STEPS)) * LEVELS
    coded = jnp.clip(jnp.round(value * up), -32767.0, 32767.0)
    out_ref[:rows, :] = coded.astype(jnp.int32).astype(jnp.int16)
    scale = jnp.broadcast_to(code.astype(jnp.int32), (PAD, value.shape[1]))
    out_ref[rows:, :] = scale.astype(jnp.int16)


def decode(ref):
    rows = ref.shape[0] - PAD
    code = ref[rows:, :].astype(jnp.int32).astype(jnp.float32)[:1]
    down = jnp.exp2(code * (1.0 / STEPS)) * (1.0 / LEVELS)
    return ref[:rows, :].astype(jnp.int32).astype(jnp.float32) * down


def iotas(rows, cols):
    return (
        lax.broadcasted_iota(jnp.int32, (rows, cols), 0),
        lax.broadcasted_iota(jnp.int32, (rows, cols), 1),
    )


def flip_matrix(octet_flip):
    row, col = iotas(G, G)
    a, x, y = row >> 6, (row >> 3) & 7, row & 7
    source = ((a ^ octet_flip) << 6) | (y << 3) | x
    return (col == source).astype(jnp.float32).astype(jnp.bfloat16)


def own_pairs():
    row, col = iotas(G, 256)
    q = row - 64
    octet, d, x = q >> 5, ((q >> 3) & 3) + 1, q & 7
    low = row < 64
    i = jnp.where(low, row >> 3, octet * 8 + x)
    j = jnp.where(low, 8 + (row & 7), octet * 8 + ((x + d) & 7))
    return i, j, col


def dot(a, b):
    return jnp.dot(a, b, preferred_element_type=jnp.float32)


def split_kernel(meta, t_ref, *outs):
    g, zh = meta[1], meta[2]
    for d in (1, 2, 3):
        stay, go = outs[2 * (d - 1)], outs[2 * (d - 1) + 1]
        p = g ^ d
        s = meta[2 + d]
        for a in range(2):
            for x in range(OCT):
                both = t_ref[a * OCT + x, pl.ds(pl.multiple_of(p * 16, 16), 16), :].astype(jnp.float32)
                first, second = both[:OCT], both[OCT:]
                take = (a ^ s) == 0
                keep = jnp.where(take, first, second)
                other = jnp.where(take, second, first)
                at = a * 64 + x * OCT
                if x % 2 == 0:
                    keep0, other0 = keep, other
                else:
                    stay[at - OCT : at + OCT, :] = jnp.concatenate([keep0, keep]).astype(jnp.bfloat16)
                    go[at - OCT : at + OCT, :] = jnp.concatenate([other0, other]).astype(jnp.bfloat16)
    own = t_ref[:, pl.ds(pl.multiple_of(g * 16, 16), 16), :].reshape(256, t_ref.shape[2])
    i, j, col = own_pairs()
    for out, source in ((outs[6], i * 16 + j), (outs[7], j * 16 + i)):
        pick = (col == source).astype(jnp.float32).astype(jnp.bfloat16)
        out[...] = dot(pick, own).astype(jnp.bfloat16)


def partial_kernel(groups, kinds, meta, lab, *refs):
    n = len(groups)
    xs, ys, v_ref = refs[:n], refs[n : 2 * n], refs[2 * n]
    outs = refs[2 * n + 1 : 2 * n + 4]
    lhs, vbuf, acc, todo, sems = refs[2 * n + 4 :]
    width = v_ref.shape[0]
    runs = width // RUN
    k = meta[0]
    zh = meta[2]
    rows = [lab[k * runs + r] for r in range(runs)]

    def tile(s, c, r):
        at = (pl.ds(pl.multiple_of(r * RUN, RUN), RUN), pl.ds(pl.multiple_of(s * width + c * RUN, RUN), RUN))
        return pltpu.make_async_copy(v_ref.at[at], vbuf.at[at], sems.at[s])

    ends = [jnp.int32(0)]
    for s in range(3):
        block = lax.rem(k + s, 32)

        def column(c, count, s=s, block=block):
            label = lab[block * runs + c]
            first = sum((row < label).astype(jnp.int32) for row in rows)
            last = first + sum((row == label).astype(jnp.int32) for row in rows)

            def one(r, count):
                tile(s, c, r).start()
                todo[count] = c * 16 + r
                return count + 1

            return lax.fori_loop(first, last, one, count)

        ends.append(lax.fori_loop(0, runs, column, ends[-1]))

    for at, d in enumerate(groups):
        x, y = xs[at][...], ys[at][...]
        if d >= 2:
            x, y = jnp.where(zh == 1, y, x), jnp.where(zh == 1, x, y)
        if d >= 1:
            y = dot(flip_matrix(meta[2 + d]), y).astype(jnp.bfloat16)
        y = -y
        for r in range(runs):
            lhs[at * G : (at + 1) * G, 2 * r * RUN : (2 * r + 1) * RUN] = x[:, r * RUN : (r + 1) * RUN]
            lhs[at * G : (at + 1) * G, (2 * r + 1) * RUN : (2 * r + 2) * RUN] = y[:, r * RUN : (r + 1) * RUN]
    acc[...] = jnp.zeros_like(acc)

    for s in range(3):
        start, end = ends[s], ends[s + 1]

        def arrived(_, c, s=s):
            tile(s, 0, 0).wait()
            return c

        lax.fori_loop(start, end, arrived, 0)

        def several(base, many, s=s):
            got = []
            for u in range(many):
                entry = todo[base + u]
                c, r = entry >> 4, entry & 15
                right = vbuf[
                    pl.ds(pl.multiple_of(r * RUN, RUN), RUN), pl.ds(pl.multiple_of(s * width + c * RUN, RUN), RUN)
                ]
                left = lhs[:, pl.ds(pl.multiple_of(r * 2 * RUN, 2 * RUN), 2 * RUN)]
                got.append((c, dot(left, jnp.concatenate([right, right], axis=0))))
            for c, value in got:
                acc[s, :, pl.ds(pl.multiple_of(c * RUN, RUN), RUN)] += value

        fours = (end - start) >> 2

        def four(at, carry, start=start):
            several(start + at * 4, 4)
            return carry

        def single(at, carry):
            several(at, 1)
            return carry

        lax.fori_loop(0, fours, four, 0)
        lax.fori_loop(start + fours * 4, end, single, 0)
        if kinds[s]:
            encode(acc[s], outs[s])
        else:
            outs[s][...] = acc[s]


def merge_kernel(meta, mine_ref, got_ref, out_ref):
    encode(mine_ref[...] + jnp.where(meta[2] == 0, decode(got_ref), 0.0), out_ref)


def finish_kernel(sent, meta, mine_ref, one_ref, two_ref, energy_ref, sums_ref, *outs):
    one = decode(one_ref)
    if sent == "cross":
        one = jnp.where(meta[2] == 1, one, 0.0)
    value = mine_ref[...] + one + decode(two_ref)
    below = energy_ref[...] - sums_ref[:, :1]
    value = value / below
    outs[0][...] = value
    if sent == "cross":
        encode(value, outs[1])
    else:
        encode(value[G:], outs[1])


def thirds(value):
    high = value.astype(jnp.bfloat16)
    rest = value - high.astype(jnp.float32)
    middle = rest.astype(jnp.bfloat16)
    low = (rest - middle.astype(jnp.float32)).astype(jnp.bfloat16)
    return jnp.concatenate([high, middle, low], axis=0)


def assemble_kernel(meta, near_ref, second_ref, third_ref, got1, got2, got3, out_ref):
    g, zh = meta[1], meta[2]
    near = near_ref[:G]
    row, col = iotas(256, G)
    i, j = row >> 4, row & 15
    oi, oj, xi, xj = i >> 3, j >> 3, i & 7, j & 7
    gap = (xj - xi) & 7
    up = 64 + oi * 32 + (gap - 1) * 8 + xi
    down = 64 + oi * 32 + (7 - gap) * 8 + xj
    same = oi == oj
    plus = jnp.where(same, jnp.where((gap >= 1) & (gap <= 4), up, -1), jnp.where(oi < oj, xi * 8 + xj, -1))
    minus = jnp.where(same, jnp.where(gap >= 5, down, -1), jnp.where(oi > oj, xj * 8 + xi, -1))
    pick = (col == plus).astype(jnp.float32) - (col == minus).astype(jnp.float32)
    pick = pick.astype(jnp.bfloat16)
    pick = jnp.concatenate([pick, pick, pick], axis=1)
    out_ref[:, pl.ds(pl.multiple_of(g * 16, 16), 16), :] = dot(pick, thirds(near)).reshape(16, 16, -1)
    for d, mine, got in ((1, near_ref[G:], got1), (2, second_ref[...], got2), (3, third_ref[...], got3)):
        p = g ^ d
        w = meta[5 + d]
        got = decode(got)
        straight, turned = mine, got
        if d >= 2:
            straight, turned = jnp.where(zh == 1, got, mine), jnp.where(zh == 1, mine, got)
        flip = flip_matrix(1 - w)
        turned = -dot(jnp.concatenate([flip, flip, flip], axis=1), thirds(turned))
        for a in range(2):
            for x in range(OCT):
                at = a * 64 + x * OCT
                o = a ^ w
                out_ref[a * OCT + x, pl.ds(pl.multiple_of(p * 16 + o * OCT, OCT), OCT), :] = straight[at : at + OCT]
                out_ref[a * OCT + x, pl.ds(pl.multiple_of(p * 16 + (1 - o) * OCT, OCT), OCT), :] = turned[at : at + OCT]


def call(kernel, name, outs, args, scratch=(), anywhere=(), flops=0, moved=0):
    specs = []
    for at, arg in enumerate(args):
        if at in anywhere:
            specs.append(pl.BlockSpec(memory_space=pl.ANY))
        elif arg.dtype == jnp.int32:
            specs.append(pl.BlockSpec(memory_space=pltpu.SMEM))
        else:
            specs.append(pl.BlockSpec(memory_space=pltpu.VMEM))
    return pl.pallas_call(
        kernel,
        out_shape=outs,
        in_specs=specs,
        out_specs=[pl.BlockSpec(memory_space=pltpu.VMEM)] * len(outs),
        scratch_shapes=scratch,
        compiler_params=pltpu.CompilerParams(vmem_limit_bytes=VMEM),
        cost_estimate=pl.CostEstimate(flops=flops, bytes_accessed=moved, transcendentals=0),
        name=name,
    )(*args)


def partials(name, groups, kinds, meta, labels, xs, ys, integrals):
    rows, width = G * len(groups), integrals.shape[0]
    outs = [
        jax.ShapeDtypeStruct((rows + PAD, width), jnp.int16) if kind else jax.ShapeDtypeStruct((rows, width), jnp.float32)
        for kind in kinds
    ]
    return call(
        functools.partial(partial_kernel, groups, kinds),
        name,
        outs,
        (meta, labels, *xs, *ys, integrals),
        scratch=[
            pltpu.VMEM((rows, 2 * width), jnp.bfloat16),
            pltpu.VMEM(integrals.shape, jnp.bfloat16),
            pltpu.VMEM((3, rows, width), jnp.float32),
            pltpu.SMEM((448,), jnp.int32),
            pltpu.SemaphoreType.DMA((3,)),
        ],
        anywhere=(2 + 2 * len(groups),),
        flops=2 * rows * width * width,
        moved=16 * 1024 * 1024,
    )


def per_device(amplitudes, integrals, pair_irrep, pair_energy, occ_energy):
    i_local, nocc, width = amplitudes.shape
    k = lax.axis_index("blk")
    g = lax.axis_index("occ")
    zh = k & 1
    w = [g & 1, g >> 1, g >> 1]
    s = [w[0], w[1] ^ zh, w[2] ^ zh]
    meta = jnp.stack([k, g, zh, *s, *w]).astype(jnp.int32)
    labels = pair_irrep.reshape(-1, RUN)[:, 0]

    own = occ_energy.reshape(4, 16)
    mine = lax.dynamic_index_in_dim(own, g, 0, keepdims=False)
    sums = []
    ii = jnp.array([i for i in range(8) for j in range(8)] + [a * 8 + x for a in range(2) for d in range(1, 5) for x in range(8)])
    jj = jnp.array([8 + j for i in range(8) for j in range(8)] + [a * 8 + (x + d) % 8 for a in range(2) for d in range(1, 5) for x in range(8)])
    sums.append(mine[ii] + mine[jj])
    for d in (1, 2, 3):
        theirs = lax.dynamic_index_in_dim(own, g ^ d, 0, keepdims=False)
        turn = zh if d >= 2 else 0
        x = jnp.where(turn == 1, theirs, mine).reshape(2, 8)
        y = jnp.where(turn == 1, mine, theirs).reshape(2, 8)
        y = jnp.where(s[d - 1] == 1, y[::-1], y)
        sums.append((x[:, :, None] + y[:, None, :]).reshape(G))
    sums = [jnp.broadcast_to(one[:, None], (G, RUN)) for one in sums]
    energy = pair_energy.reshape(1, width)

    slab = jax.ShapeDtypeStruct((G, width), jnp.bfloat16)
    stay1, go1, stay2, go2, stay3, go3, own_x, own_y = call(
        split_kernel, "split", [slab] * 8, (meta, amplitudes), moved=6 * 1024 * 1024
    )
    got2 = send(go2, lambda b, o: (b, o ^ 2))
    got3 = send(go3, lambda b, o: (b, o ^ 3))
    got1 = send(go1, lambda b, o: (b, o ^ 1))

    near0, near1, near2 = partials("near", (0, 1), (0, 1, 1), meta, labels, (own_x, stay1), (own_y, got1), integrals)
    near1 = send(near1, lambda b, o: (b + 1, o))
    near2 = send(near2, lambda b, o: (b + 2, o))

    coded = [jax.ShapeDtypeStruct((G + PAD, width), jnp.int16)]
    crossed = []
    for d, stay, got in ((2, stay2, got2), (3, stay3, got3)):
        far0, far1, far2 = partials("far%d" % d, (d,), (0, 1, 0), meta, labels, (stay,), (got,), integrals)
        far1 = send(far1, lambda b, o, d=d: (b ^ 1, o ^ d))
        (far2,) = call(merge_kernel, "merge%d" % d, coded, (meta, far2, far1), moved=2 * 1024 * 1024)
        far2 = send(far2, lambda b, o: (b + 2, o))
        crossed.append((far0, far1, far2))

    done, back = [], []
    for d, (far0, far1, far2) in ((2, crossed[0]), (3, crossed[1])):
        value, code = call(
            functools.partial(finish_kernel, "cross"),
            "finish%d" % d,
            [jax.ShapeDtypeStruct((G, width), jnp.float32)] + coded,
            (meta, far0, far1, far2, energy, sums[d]),
            moved=4 * 1024 * 1024,
        )
        done.append(value)
        back.append(send(code, lambda b, o, d=d: (b, o ^ d)))
    near, code = call(
        functools.partial(finish_kernel, "near"),
        "finish1",
        [jax.ShapeDtypeStruct((2 * G, width), jnp.float32)] + coded,
        (meta, near0, near1, near2, energy, jnp.concatenate(sums[:2])),
        moved=6 * 1024 * 1024,
    )
    back1 = send(code, lambda b, o: (b, o ^ 1))
    (out,) = call(
        assemble_kernel,
        "assemble",
        [jax.ShapeDtypeStruct((i_local, nocc, width), jnp.float32)],
        (meta, near, done[0], done[1], back1, back[0], back[1]),
        moved=12 * 1024 * 1024,
    )
    return out


def solution(mesh):
    placed = (P("occ", None, "blk"), P("blk", None), P(), P("blk"), P())
    return jax.shard_map(
        per_device, mesh=mesh, in_specs=placed, out_specs=P("occ", None, "blk"), check_vma=False
    )
```

```python
import functools

import jax
import jax.numpy as jnp
from jax import lax
from jax.experimental import pallas as pl
from jax.experimental.pallas import tpu as pltpu
from jax.sharding import PartitionSpec as P

BOTH = ("blk", "occ")
BLOCKS = 32
RUN = 128
OCT = 8
G = 128
PAD = 16
LEVELS = 32000.0
STEPS = 256.0
MANY = 8
SLOTS = 160
MIB = 1024 * 1024
ANY = pl.BlockSpec(memory_space=pl.ANY)
IN_VMEM = pl.BlockSpec(memory_space=pltpu.VMEM)
IN_SMEM = pl.BlockSpec(memory_space=pltpu.SMEM)
TOKEN = jax.ShapeDtypeStruct((8,), jnp.int32)


def routes(where):
    pairs = []
    for blk in range(BLOCKS):
        for occ in range(4):
            to_blk, to_occ = where(blk, occ)
            pairs.append((blk * 4 + occ, (to_blk % BLOCKS) * 4 + to_occ))
    return pairs


def send(value, where):
    return lax.ppermute(value, BOTH, routes(where))


def place():
    k = lax.axis_index("blk")
    return k, lax.axis_index("occ"), lax.rem(k, 2)


def later(g, d):
    return lax.rem(g, 2) if d == 1 else lax.div(g, 2)


def side(g, zh, d):
    return later(g, d) if d == 1 else lax.rem(later(g, d) + zh, 2)


def apart(g, d):
    low, high = lax.rem(g, 2), lax.div(g, 2)
    low = 1 - low if d & 1 else low
    high = 1 - high if d & 2 else high
    return high * 2 + low


def encode(value, out_ref):
    rows = value.shape[0]
    most = jnp.max(jnp.abs(value), axis=0, keepdims=True)
    code = jnp.ceil(jnp.log2(jnp.maximum(most, 2.0**-120)) * STEPS)
    up = jnp.exp2(code * (-1.0 / STEPS)) * LEVELS
    coded = jnp.clip(jnp.round(value * up), -32767.0, 32767.0)
    out_ref[:rows, :] = coded.astype(jnp.int32).astype(jnp.int16)
    scale = jnp.broadcast_to(code.astype(jnp.int32), (PAD, value.shape[1]))
    out_ref[rows:, :] = scale.astype(jnp.int16)


def scales(ref):
    code = ref[ref.shape[0] - PAD :, :].astype(jnp.int32).astype(jnp.float32)[:1]
    return jnp.exp2(code * (1.0 / STEPS)) * (1.0 / LEVELS)


def codes(ref):
    return ref[: ref.shape[0] - PAD, :].astype(jnp.int32)


def decode(ref):
    return codes(ref).astype(jnp.float32) * scales(ref)


def iotas(rows, cols):
    return (
        lax.broadcasted_iota(jnp.int32, (rows, cols), 0),
        lax.broadcasted_iota(jnp.int32, (rows, cols), 1),
    )


def ones_at(where):
    return where.astype(jnp.float32).astype(jnp.bfloat16)


def flip_matrix(octet_flip):
    row, col = iotas(G, G)
    a, x, y = row >> 6, (row >> 3) & 7, row & 7
    return ones_at(col == (((a ^ octet_flip) << 6) | (y << 3) | x))


def own_pairs(cols):
    row, col = iotas(G, cols)
    q = row - 64
    octet, d, x = q >> 5, ((q >> 3) & 3) + 1, q & 7
    low = row < 64
    i = jnp.where(low, row >> 3, octet * 8 + x)
    j = jnp.where(low, 8 + (row & 7), octet * 8 + ((x + d) & 7))
    return i, j, col


def dot(a, b):
    return jnp.dot(a, b, preferred_element_type=jnp.float32)


def thirds(value):
    high = value.astype(jnp.bfloat16)
    rest = value - high.astype(jnp.float32)
    middle = rest.astype(jnp.bfloat16)
    low = (rest - middle.astype(jnp.float32)).astype(jnp.bfloat16)
    return jnp.concatenate([high, middle, low], axis=0)


def thrice(matrix):
    return jnp.concatenate([matrix, matrix, matrix], axis=1)


def slab(t_ref, group):
    return t_ref.at[:, pl.ds(pl.multiple_of(group * 16, 16), 16), :]


def half(both, s):
    parts = []
    for a in range(2):
        for x in range(OCT):
            one = both[a * OCT + x].astype(jnp.float32)
            parts.append(jnp.where((a ^ s) == 0, one[:OCT], one[OCT:]))
    return jnp.concatenate(parts, axis=0).astype(jnp.bfloat16)


def split_kernel(ds, t_ref, *refs):
    outs, (buf, sems) = refs[: len(ds)], refs[len(ds) :]
    _, g, zh = place()
    loads = [pltpu.make_async_copy(slab(t_ref, apart(g, d)), buf.at[at], sems.at[at]) for at, d in enumerate(ds)]
    for load in loads:
        load.start()
    for at, d in enumerate(ds):
        loads[at].wait()
        outs[at][...] = half(buf[at], 1 - side(g, zh, d))


def plan_kernel(lab, todo):
    k, _, _ = place()
    runs = lab.shape[0] // BLOCKS
    rows = [lab[k * runs + r] for r in range(runs)]
    for s in range(3):
        block = lax.rem(k + s, BLOCKS)
        base = 8 + s * SLOTS

        def column(c, count, block=block, base=base):
            label = lab[block * runs + c]
            first = sum((row < label).astype(jnp.int32) for row in rows)
            last = first + sum((row == label).astype(jnp.int32) for row in rows)

            def one(r, count):
                todo[base + count] = c * 256 + r * 16 + c
                return count + 1

            return lax.fori_loop(first, last, one, count)

        count = lax.fori_loop(0, runs, column, jnp.int32(0))
        todo[s] = count

        def fill(at, carry, base=base, count=count):
            todo[base + at] = runs * 256 + lax.rem(todo[base + count - 1], 256)
            return carry

        lax.fori_loop(count, lax.div(count + MANY - 1, MANY) * MANY, fill, 0)


def partial_kernel(groups, offsets, todo, *refs):
    n = len(groups)
    if n:
        t_ref, *refs = refs
        partners = sum(d > 0 for d in groups)
        got, refs = refs[:partners], refs[partners:]
    else:
        lhs, *refs = refs
    v_ref, _, *refs = refs
    outs, refs = refs[: len(offsets)], refs[len(offsets) :]
    if n:
        lhs, *refs = refs
    token, vbuf, acc, sems, *refs = refs
    width = v_ref.shape[0]
    runs = width // RUN
    k, g, zh = place()
    token[0] = k

    def tile(s, at, entry):
        r, c = lax.rem(lax.div(entry, 16), 16), lax.rem(entry, 16)
        source = v_ref.at[
            pl.ds(pl.multiple_of(r * RUN, RUN), RUN), pl.ds(pl.multiple_of(s * width + c * RUN, RUN), RUN)
        ]
        return source

    for at, (s, _) in enumerate(offsets):

        def begin(e, carry, at=at, s=s):
            source = tile(s, at, todo[8 + s * SLOTS + e])
            pltpu.make_async_copy(source, vbuf.at[at, e], sems.at[at]).start()
            return carry

        lax.fori_loop(0, todo[s], begin, 0)

    if n:
        tbuf, gbuf, load_sems = refs
        loads = []
        take = 0
        for at, d in enumerate(groups):
            load = [pltpu.make_async_copy(slab(t_ref, apart(g, d) if d else g), tbuf.at[at], load_sems.at[2 * at])]
            if d:
                load.append(pltpu.make_async_copy(got[take], gbuf.at[at], load_sems.at[2 * at + 1]))
                take += 1
            for one in load:
                one.start()
            loads.append(load)
        acc[...] = jnp.zeros_like(acc)
        for at, d in enumerate(groups):
            for one in loads[at]:
                one.wait()
            if d:
                s = side(g, zh, d)
                x, y = half(tbuf[at], s), gbuf[at]
                if d >= 2:
                    x, y = jnp.where(zh == 1, y, x), jnp.where(zh == 1, x, y)
                y = -dot(flip_matrix(s), y)
            else:
                own = tbuf[at].reshape(256, width)
                i, j, col = own_pairs(256)
                x = dot(ones_at(col == i * 16 + j), own).astype(jnp.bfloat16)
                y = -dot(ones_at(col == j * 16 + i), own)
            y = y.astype(jnp.bfloat16)
            for r in range(runs):
                lhs[at * G : (at + 1) * G, 2 * r * RUN : (2 * r + 1) * RUN] = x[:, r * RUN : (r + 1) * RUN]
                lhs[at * G : (at + 1) * G, (2 * r + 1) * RUN : (2 * r + 2) * RUN] = y[:, r * RUN : (r + 1) * RUN]
    else:
        acc[...] = jnp.zeros_like(acc)

    for at, (s, coded) in enumerate(offsets):

        def arrived(e, carry, at=at, s=s):
            pltpu.make_async_copy(tile(s, at, 0), vbuf.at[at, e], sems.at[at]).wait()
            return carry

        lax.fori_loop(0, todo[s], arrived, 0)

        def several(step, carry, at=at, s=s):
            products = []
            for u in range(MANY):
                e = step * MANY + u
                entry = todo[8 + s * SLOTS + e]
                c, r = lax.div(entry, 256), lax.rem(lax.div(entry, 16), 16)
                right = vbuf[at, jnp.minimum(e, todo[s] - 1)]
                left = lhs[:, pl.ds(pl.multiple_of(r * 2 * RUN, 2 * RUN), 2 * RUN)]
                products.append((c, dot(left, jnp.concatenate([right, right], axis=0))))
            for c, value in products:
                acc[at, :, pl.ds(pl.multiple_of(c * RUN, RUN), RUN)] += value
            return carry

        lax.fori_loop(0, lax.div(todo[s] + MANY - 1, MANY), several, 0)
        if coded:
            encode(acc[at, :, :width], outs[at])
        else:
            outs[at][...] = acc[at, :, :width]


def fetch(pairs, sems):
    copies = [pltpu.make_async_copy(a, b, sems.at[at]) for at, (a, b) in enumerate(pairs)]
    for copy in copies:
        copy.start()
    for copy in copies:
        copy.wait()


def merge_kernel(mine_ref, got_ref, out_ref, buf, sems):
    fetch([(got_ref, buf)], sems)
    _, _, zh = place()
    encode(mine_ref[...] + jnp.where(zh == 0, decode(buf), 0.0), out_ref)


def finish_kernel(ds, mine_ref, one_ref, two_ref, energy_ref, occ_ref, value_ref, code_ref, one, two, sems):
    fetch([(one_ref, one), (two_ref, two)], sems)
    _, g, zh = place()
    sums = []
    occ = thirds(occ_ref[...])
    for d in ds:
        if d:
            s = side(g, zh, d)
            row, col = iotas(G, 64)
            a, x, y = row >> 6, (row >> 3) & 7, row & 7
            p = apart(g, d)
            first, second = (g, p) if d == 1 else (jnp.where(zh == 1, p, g), jnp.where(zh == 1, g, p))
            i, j = a * OCT + x + first * 16, (a ^ s) * OCT + y + second * 16
        else:
            i, j, col = own_pairs(64)
            i, j = i + g * 16, j + g * 16
        pick = (col == i).astype(jnp.float32) + (col == j).astype(jnp.float32)
        sums.append(dot(thrice(pick.astype(jnp.bfloat16)), occ)[:, :1])
    sums = jnp.concatenate(sums, axis=0) if len(sums) > 1 else sums[0]
    first = decode(one)
    if ds[-1] >= 2:
        first = jnp.where(zh == 1, first, 0.0)
    value = (mine_ref[...] + first + decode(two)) / (energy_ref[...] - sums)
    value_ref[...] = value
    encode(value[-G:], code_ref)


def put(out_ref, buf, value, d, w, turned, g, sems, at):
    p = apart(g, d)
    copies = []
    buf[at] = value.reshape(2, OCT, OCT, value.shape[1])
    for a in range(2):
        o = p * 2 + lax.rem(a + w + turned, 2)
        copy = pltpu.make_async_copy(
            buf.at[at, a],
            out_ref.at[a * OCT : (a + 1) * OCT, pl.ds(pl.multiple_of(o * OCT, OCT), OCT), :],
            sems.at[at, a],
        )
        copy.start()
        copies.append(copy)
    return copies


def returned(ref, d, w, zh):
    code = codes(ref)
    pieces = jnp.concatenate(
        [(code >> 8).astype(jnp.float32).astype(jnp.bfloat16), (code & 255).astype(jnp.float32).astype(jnp.bfloat16)]
    )
    flip = flip_matrix(1 - w).astype(jnp.float32)
    turned = dot(jnp.concatenate([flip * -256.0, -flip], axis=1).astype(jnp.bfloat16), pieces)
    if d == 1:
        return turned * scales(ref), 1
    return jnp.where(zh == 1, code.astype(jnp.float32), turned) * scales(ref), 1 - zh


def own_kernel(near_ref, second_ref, third_ref, got1_ref, out_ref, got1, square, buf, sems, load_sems):
    load = pltpu.make_async_copy(got1_ref, got1, load_sems.at[0])
    load.start()
    _, g, zh = place()
    copies = []
    for at, (d, mine) in enumerate(((2, second_ref[...]), (3, third_ref[...]), (1, near_ref[G:]))):
        w = later(g, d)
        if d == 1:
            copies += put(out_ref, buf, mine, d, w, 0, g, sems, at)
        else:
            turned = -dot(thrice(flip_matrix(1 - w)), thirds(mine))
            copies += put(out_ref, buf, jnp.where(zh == 1, turned, mine), d, w, zh, g, sems, at)
    row, col = iotas(256, G)
    i, j = row >> 4, row & 15
    oi, oj, xi, xj = i >> 3, j >> 3, i & 7, j & 7
    gap = (xj - xi) & 7
    up = 64 + oi * 32 + (gap - 1) * 8 + xi
    down = 64 + oi * 32 + (7 - gap) * 8 + xj
    same = oi == oj
    plus = jnp.where(same, jnp.where((gap >= 1) & (gap <= 4), up, -1), jnp.where(oi < oj, xi * 8 + xj, -1))
    minus = jnp.where(same, jnp.where(gap >= 5, down, -1), jnp.where(oi > oj, xj * 8 + xi, -1))
    pick = (col == plus).astype(jnp.float32) - (col == minus).astype(jnp.float32)
    square[...] = dot(thrice(pick.astype(jnp.bfloat16)), thirds(near_ref[:G])).reshape(square.shape)
    copy = pltpu.make_async_copy(square, slab(out_ref, g), load_sems.at[1])
    copy.start()
    copies.append(copy)
    load.wait()
    w = later(g, 1)
    value, turned = returned(got1, 1, w, zh)
    copies += put(out_ref, buf, value, 1, w, turned, g, sems, 3)
    for copy in copies:
        copy.wait()


def back_kernel(d, got_ref, _, out_ref, got, buf, sems, load_sems):
    fetch([(got_ref, got)], load_sems)
    _, g, zh = place()
    w = later(g, d)
    value, turned = returned(got, d, w, zh)
    for copy in put(out_ref, buf, value, d, w, turned, g, sems, 0):
        copy.wait()


def call(kernel, name, outs, args, in_specs, out_specs, scratch=(), flops=0, moved=0, aliases={}, room=12):
    return pl.pallas_call(
        kernel,
        out_shape=outs,
        in_specs=in_specs,
        out_specs=out_specs,
        scratch_shapes=scratch,
        input_output_aliases=aliases,
        compiler_params=pltpu.CompilerParams(vmem_limit_bytes=room * MIB),
        cost_estimate=pl.CostEstimate(flops=flops, bytes_accessed=moved, transcendentals=0),
        name=name,
    )(*args)


def plain(rows, width):
    return jax.ShapeDtypeStruct((rows, width), jnp.float32)


def coded(rows, width):
    return jax.ShapeDtypeStruct((rows + PAD, width), jnp.int16)


def partials(name, groups, offsets, todo, rows, integrals, token, amplitudes=None, got=(), lhs=None):
    width = integrals.shape[0]
    outs = [coded(rows, width) if as_code else plain(rows, width) for _, as_code in offsets]
    scratch = [
        pltpu.VMEM((len(offsets), 144, RUN, RUN), jnp.bfloat16),
        pltpu.VMEM((len(offsets), rows, width + RUN), jnp.float32),
        pltpu.SemaphoreType.DMA((len(offsets),)),
    ]
    if groups:
        args = (todo, amplitudes, *got, integrals, token)
        specs = [IN_SMEM] + [ANY] * (2 + len(got)) + [IN_SMEM]
        outs.append(jax.ShapeDtypeStruct((rows, 2 * width), jnp.bfloat16))
        scratch += [
            pltpu.VMEM((len(groups), 16, 16, width), jnp.bfloat16),
            pltpu.VMEM((len(groups), G, width), jnp.bfloat16),
            pltpu.SemaphoreType.DMA((2 * len(groups),)),
        ]
    else:
        args = (todo, lhs, integrals, token)
        specs = [IN_SMEM, IN_VMEM, ANY, IN_SMEM]
    return call(
        functools.partial(partial_kernel, groups, offsets),
        name,
        outs + [TOKEN],
        args,
        specs,
        [IN_VMEM] * len(outs) + [IN_SMEM],
        scratch,
        flops=len(offsets) * rows * width * width // 2,
        moved=4 * 1024 * 1024,
        room=26,
    )


def per_device(amplitudes, integrals, pair_irrep, pair_energy, occ_energy):
    i_local, nocc, width = amplitudes.shape
    labels = pair_irrep.reshape(-1, RUN)[:, 0]
    energy = pair_energy.reshape(1, width)
    occ = jnp.broadcast_to(occ_energy[:, None], (nocc, RUN))

    def split(ds):
        return call(
            functools.partial(split_kernel, ds),
            "split" + "".join(map(str, ds)),
            [jax.ShapeDtypeStruct((G, width), jnp.bfloat16)] * len(ds),
            (amplitudes,),
            [ANY],
            [IN_VMEM] * len(ds),
            [pltpu.VMEM((len(ds), 16, 16, width), jnp.bfloat16), pltpu.SemaphoreType.DMA((len(ds),))],
            moved=2 * 1024 * 1024,
        )

    (go2,) = split((2,))
    got2 = send(go2, lambda b, o: (b, o ^ 2))
    go3, go1 = split((3, 1))
    got3 = send(go3, lambda b, o: (b, o ^ 3))
    got1 = send(go1, lambda b, o: (b, o ^ 1))
    (todo,) = call(
        plan_kernel,
        "plan",
        [jax.ShapeDtypeStruct((8 + 3 * SLOTS,), jnp.int32)],
        (labels,),
        [IN_SMEM],
        [IN_SMEM],
        moved=1024 * 1024,
    )

    near1, near2, near_rows, token = partials(
        "near", (0, 1), ((1, 1), (2, 1)), todo, 2 * G, integrals, todo, amplitudes, (got1,)
    )
    near1 = send(near1, lambda b, o: (b + 1, o))
    near2 = send(near2, lambda b, o: (b + 2, o))

    far = {}
    for d, got in ((2, got2), (3, got3)):
        far1, rows, token = partials("far%d" % d, (d,), ((1, 1),), todo, G, integrals, token, amplitudes, (got,))
        far[d] = send(far1, lambda b, o, d=d: (b ^ 1, o ^ d)), rows
    base = {}
    for d in (2, 3):
        far2, far0, token = partials("rest%d" % d, (), ((2, 0), (0, 0)), todo, G, integrals, token, lhs=far[d][1])
        base[d] = far0, far2
    near0, token = partials("rest1", (), ((0, 0),), todo, 2 * G, integrals, token, lhs=near_rows)

    onward = {}
    for d in (2, 3):
        far1, _ = far[d]
        (far2,) = call(
            merge_kernel,
            "merge%d" % d,
            [coded(G, width)],
            (base[d][1], far1),
            [IN_VMEM, ANY],
            [IN_VMEM],
            [pltpu.VMEM((G + PAD, width), jnp.int16), pltpu.SemaphoreType.DMA((1,))],
            moved=2 * 1024 * 1024,
        )
        onward[d] = send(far2, lambda b, o: (b + 2, o))

    def finish(name, ds, mine, one, two):
        rows = G * len(ds)
        return call(
            functools.partial(finish_kernel, ds),
            name,
            [plain(rows, width), coded(G, width)],
            (mine, one, two, energy, occ),
            [IN_VMEM, ANY, ANY, IN_VMEM, IN_VMEM],
            [IN_VMEM] * 2,
            [
                pltpu.VMEM((rows + PAD, width), jnp.int16),
                pltpu.VMEM((rows + PAD, width), jnp.int16),
                pltpu.SemaphoreType.DMA((2,)),
            ],
            moved=2 * 1024 * 1024,
        )

    done, back = {}, {}
    for d in (2, 3):
        done[d], code = finish("finish%d" % d, (d,), base[d][0], far[d][0], onward[d])
        back[d] = send(code, lambda b, o, d=d: (b, o ^ d))
    near, code = finish("finish1", (0, 1), near0, near1, near2)
    back1 = send(code, lambda b, o: (b, o ^ 1))

    out = jax.ShapeDtypeStruct((i_local, nocc, width), jnp.float32)
    landed = pltpu.VMEM((G + PAD, width), jnp.int16)
    (whole,) = call(
        own_kernel,
        "own",
        [out],
        (near, done[2], done[3], back1),
        [IN_VMEM, IN_VMEM, IN_VMEM, ANY],
        [ANY],
        [
            landed,
            pltpu.VMEM((16, 16, width), jnp.float32),
            pltpu.VMEM((4, 2, OCT, OCT, width), jnp.float32),
            pltpu.SemaphoreType.DMA((4, 2)),
            pltpu.SemaphoreType.DMA((2,)),
        ],
        moved=6 * 1024 * 1024,
        room=24,
    )
    for d in (2, 3):
        (whole,) = call(
            functools.partial(back_kernel, d),
            "back%d" % d,
            [out],
            (back[d], whole),
            [ANY, ANY],
            [ANY],
            [
                landed,
                pltpu.VMEM((1, 2, OCT, OCT, width), jnp.float32),
                pltpu.SemaphoreType.DMA((1, 2)),
                pltpu.SemaphoreType.DMA((1,)),
            ],
            moved=2 * 1024 * 1024,
            aliases={1: 0},
        )
    return whole


def solution(mesh):
    placed = (P("occ", None, "blk"), P("blk", None), P(), P("blk"), P())
    return jax.shard_map(
        per_device, mesh=mesh, in_specs=placed, out_specs=P("occ", None, "blk"), check_vma=False
    )
```

```python
import functools

import jax
import jax.numpy as jnp
from jax import lax
from jax.experimental import pallas as pl
from jax.experimental.pallas import tpu as pltpu
from jax.sharding import PartitionSpec as P

BOTH = ("blk", "occ")
BLOCKS = 32
RUN = 128
OCT = 8
G = 128
PAD = 16
LEVELS = 32000.0
STEPS = 256.0
MANY = 8
LABELS = 8
SLOTS = 160
MIB = 1024 * 1024
ANY = pl.BlockSpec(memory_space=pl.ANY)
IN_VMEM = pl.BlockSpec(memory_space=pltpu.VMEM)
IN_HBM = pl.BlockSpec(memory_space=pltpu.HBM)
IN_SMEM = pl.BlockSpec(memory_space=pltpu.SMEM)
TOKEN = jax.ShapeDtypeStruct((8,), jnp.int32)


def routes(where):
    pairs = []
    for blk in range(BLOCKS):
        for occ in range(4):
            to_blk, to_occ = where(blk, occ)
            pairs.append((blk * 4 + occ, (to_blk % BLOCKS) * 4 + to_occ))
    return pairs


def send(value, where):
    return lax.ppermute(value, BOTH, routes(where))


def place():
    k = lax.axis_index("blk")
    return k, lax.axis_index("occ"), lax.rem(k, 2)


def later(g, d):
    return lax.rem(g, 2) if d == 1 else lax.div(g, 2)


def side(g, zh, d):
    return later(g, d) if d == 1 else lax.rem(later(g, d) + zh, 2)


def apart(g, d):
    low, high = lax.rem(g, 2), lax.div(g, 2)
    low = 1 - low if d & 1 else low
    high = 1 - high if d & 2 else high
    return high * 2 + low


def encode(value, out_ref):
    rows = value.shape[0]
    most = jnp.max(jnp.abs(value), axis=0, keepdims=True)
    code = jnp.ceil(jnp.log2(jnp.maximum(most, 2.0**-120)) * STEPS)
    up = jnp.exp2(code * (-1.0 / STEPS)) * LEVELS
    coded = jnp.clip(jnp.round(value * up), -32767.0, 32767.0)
    out_ref[:rows, :] = coded.astype(jnp.int32).astype(jnp.int16)
    scale = jnp.broadcast_to(code.astype(jnp.int32), (PAD, value.shape[1]))
    out_ref[rows:, :] = scale.astype(jnp.int16)


def scales(ref):
    code = ref[ref.shape[0] - PAD :, :].astype(jnp.int32).astype(jnp.float32)[:1]
    return jnp.exp2(code * (1.0 / STEPS)) * (1.0 / LEVELS)


def codes(ref):
    return ref[: ref.shape[0] - PAD, :].astype(jnp.int32)


def decode(ref):
    return codes(ref).astype(jnp.float32) * scales(ref)


def iotas(rows, cols):
    return (
        lax.broadcasted_iota(jnp.int32, (rows, cols), 0),
        lax.broadcasted_iota(jnp.int32, (rows, cols), 1),
    )


def ones_at(where):
    return where.astype(jnp.float32).astype(jnp.bfloat16)


def flip_matrix(octet_flip):
    row, col = iotas(G, G)
    a, x, y = row >> 6, (row >> 3) & 7, row & 7
    return ones_at(col == (((a ^ octet_flip) << 6) | (y << 3) | x))


def own_pairs(cols):
    row, col = iotas(G, cols)
    q = row - 64
    octet, d, x = q >> 5, ((q >> 3) & 3) + 1, q & 7
    low = row < 64
    i = jnp.where(low, row >> 3, octet * 8 + x)
    j = jnp.where(low, 8 + (row & 7), octet * 8 + ((x + d) & 7))
    return i, j, col


def dot(a, b):
    return jnp.dot(a, b, preferred_element_type=jnp.float32)


def thirds(value):
    high = value.astype(jnp.bfloat16)
    rest = value - high.astype(jnp.float32)
    middle = rest.astype(jnp.bfloat16)
    low = (rest - middle.astype(jnp.float32)).astype(jnp.bfloat16)
    return jnp.concatenate([high, middle, low], axis=0)


def thrice(matrix):
    return jnp.concatenate([matrix, matrix, matrix], axis=1)


def slab(t_ref, group):
    return t_ref.at[:, pl.ds(pl.multiple_of(group * 16, 16), 16), :]


def half(both, s):
    parts = []
    for a in range(2):
        for x in range(OCT):
            one = both[a * OCT + x].astype(jnp.float32)
            parts.append(jnp.where((a ^ s) == 0, one[:OCT], one[OCT:]))
    return jnp.concatenate(parts, axis=0).astype(jnp.bfloat16)


def split_kernel(go, stay, own, t_ref, _, *refs):
    outs, (buf, sems) = refs[:-2], refs[-2:]
    _, g, zh = place()
    ds = sorted({*go, *stay}, reverse=True) + [0] * own
    loads = [pltpu.make_async_copy(slab(t_ref, apart(g, d) if d else g), buf.at[at], sems.at[at]) for at, d in enumerate(ds)]
    for load in loads:
        load.start()
    for load in loads:
        load.wait()
    for at, d in enumerate(go):
        outs[at][...] = half(buf[ds.index(d)], 1 - side(g, zh, d))
    for at, d in enumerate(stay):
        outs[len(go) + at][...] = half(buf[ds.index(d)], side(g, zh, d))
    if own:
        outs[-1][...] = buf[len(ds) - 1].reshape(256, buf.shape[3])


def plan_kernel(lab, todo, begins):
    k, _, _ = place()
    runs = lab.shape[0] // BLOCKS
    rows = [lab[k * runs + r] for r in range(runs)]
    for label in range(LABELS + 1):
        begins[label] = sum((row < label).astype(jnp.int32) for row in rows)
    for s in range(3):
        block = lax.rem(k + s, BLOCKS)
        base = 8 + s * SLOTS

        def column(c, count, block=block, base=base):
            label = lab[block * runs + c]

            def one(r, count):
                todo[base + count] = c * 256 + r * 16 + c
                return count + 1

            return lax.fori_loop(begins[label], begins[label + 1], one, count)

        count = lax.fori_loop(0, runs, column, jnp.int32(0))
        todo[s] = count

        def fill(at, carry, base=base, count=count):
            todo[base + at] = runs * 256 + lax.rem(todo[base + count - 1], 256)
            return carry

        lax.fori_loop(count, lax.div(count + MANY - 1, MANY) * MANY, fill, 0)


def partial_kernel(groups, offsets, after, todo, *refs):
    n = len(groups)
    if n:
        sides = []
        for d in groups:
            sides.append(refs[: 1 + (d > 0)])
            refs = refs[1 + (d > 0) :]
    else:
        lhs, *refs = refs
    v_ref, _, *refs = refs
    if after:
        _, *refs = refs
    acc, parts = refs[-2], refs[-2].shape[1] // G
    outs, refs = refs[: len(offsets) * parts], refs[len(offsets) * parts :]
    if n:
        lhs, *refs = refs
    token, vbuf, acc, sems = refs
    width = v_ref.shape[0]
    runs = width // RUN
    k, g, zh = place()
    token[0] = k

    def tile(s, entry):
        r, c = lax.rem(lax.div(entry, 16), 16), lax.rem(entry, 16)
        return v_ref.at[
            pl.ds(pl.multiple_of(r * RUN, RUN), RUN), pl.ds(pl.multiple_of(s * width + c * RUN, RUN), RUN)
        ]

    for at, (s, _) in enumerate(offsets):

        def begin(e, carry, at=at, s=s):
            source = tile(s, todo[8 + s * SLOTS + e])
            pltpu.make_async_copy(source, vbuf.at[at, e], sems.at[at]).start()
            return carry

        lax.fori_loop(0, todo[s], begin, 0)

    acc[...] = jnp.zeros_like(acc)
    for at, d in enumerate(groups):
        if d:
            s = side(g, zh, d)
            x, y = sides[at][0][...], sides[at][1][...]
            if d >= 2:
                x, y = jnp.where(zh == 1, y, x), jnp.where(zh == 1, x, y)
            y = -dot(flip_matrix(s), y)
        else:
            own = sides[at][0][...]
            i, j, col = own_pairs(256)
            x = dot(ones_at(col == i * 16 + j), own).astype(jnp.bfloat16)
            y = -dot(ones_at(col == j * 16 + i), own)
        y = y.astype(jnp.bfloat16)
        for r in range(runs):
            lhs[at * G : (at + 1) * G, 2 * r * RUN : (2 * r + 1) * RUN] = x[:, r * RUN : (r + 1) * RUN]
            lhs[at * G : (at + 1) * G, (2 * r + 1) * RUN : (2 * r + 2) * RUN] = y[:, r * RUN : (r + 1) * RUN]

    for at, (s, coded) in enumerate(offsets):

        def arrived(e, carry, at=at, s=s):
            pltpu.make_async_copy(tile(s, 0), vbuf.at[at, e], sems.at[at]).wait()
            return carry

        lax.fori_loop(0, todo[s], arrived, 0)

        def several(step, carry, at=at, s=s):
            products = []
            for u in range(MANY):
                e = step * MANY + u
                entry = todo[8 + s * SLOTS + e]
                c, r = lax.div(entry, 256), lax.rem(lax.div(entry, 16), 16)
                right = vbuf[at, jnp.minimum(e, todo[s] - 1)]
                left = lhs[:, pl.ds(pl.multiple_of(r * 2 * RUN, 2 * RUN), 2 * RUN)]
                products.append((c, dot(left, jnp.concatenate([right, right], axis=0))))
            for c, value in products:
                acc[at, :, pl.ds(pl.multiple_of(c * RUN, RUN), RUN)] += value
            return carry

        lax.fori_loop(0, lax.div(todo[s] + MANY - 1, MANY), several, 0)
        for part in range(parts):
            value = acc[at, part * G : (part + 1) * G, :width]
            if coded:
                encode(value, outs[at * parts + part])
            else:
                outs[at * parts + part][...] = value


def fetch(pairs, sems):
    copies = [pltpu.make_async_copy(a, b, sems.at[at]) for at, (a, b) in enumerate(pairs)]
    for copy in copies:
        copy.start()
    for copy in copies:
        copy.wait()


def merge_kernel(plus, mine_ref, got_ref, out_ref, buf, sems):
    fetch([(got_ref, buf)], sems)
    _, _, zh = place()
    mine = decode(mine_ref) if plus else mine_ref[...]
    encode(mine + jnp.where(zh == 0, decode(buf), 0.0), out_ref)


def finish_kernel(d, mine_ref, one_ref, two_ref, energy_ref, occ_ref, *refs):
    if d == 1:
        _, *refs = refs
    value_ref, *code_ref, one, two, sems = refs
    fetch([(one_ref, one), (two_ref, two)], sems)
    _, g, zh = place()
    if d:
        s = side(g, zh, d)
        row, col = iotas(G, 64)
        a, x, y = row >> 6, (row >> 3) & 7, row & 7
        p = apart(g, d)
        first, second = (g, p) if d == 1 else (jnp.where(zh == 1, p, g), jnp.where(zh == 1, g, p))
        i, j = a * OCT + x + first * 16, (a ^ s) * OCT + y + second * 16
    else:
        i, j, col = own_pairs(64)
        i, j = i + g * 16, j + g * 16
    pick = (col == i).astype(jnp.float32) + (col == j).astype(jnp.float32)
    sums = dot(thrice(pick.astype(jnp.bfloat16)), thirds(occ_ref[...]))[:, :1]
    first = decode(one)
    if d != 1:
        first = jnp.where(zh == 1, first, 0.0)
    value = (mine_ref[...] + first + decode(two)) / (energy_ref[...] - sums)
    value_ref[...] = value
    if d:
        encode(value, code_ref[0])


def put(out_ref, buf, value, d, w, turned, g, sems, at):
    p = apart(g, d)
    copies = []
    buf[at] = value.reshape(2, OCT, OCT, value.shape[1])
    for a in range(2):
        o = p * 2 + lax.rem(a + w + turned, 2)
        copy = pltpu.make_async_copy(
            buf.at[at, a],
            out_ref.at[a * OCT : (a + 1) * OCT, pl.ds(pl.multiple_of(o * OCT, OCT), OCT), :],
            sems.at[at, a],
        )
        copy.start()
        copies.append(copy)
    return copies


def returned(ref, d, w, zh):
    code = codes(ref)
    pieces = jnp.concatenate(
        [(code >> 8).astype(jnp.float32).astype(jnp.bfloat16), (code & 255).astype(jnp.float32).astype(jnp.bfloat16)]
    )
    flip = flip_matrix(1 - w).astype(jnp.float32)
    turned = dot(jnp.concatenate([flip * -256.0, -flip], axis=1).astype(jnp.bfloat16), pieces)
    if d == 1:
        return turned * scales(ref), 1
    return jnp.where(zh == 1, code.astype(jnp.float32), turned) * scales(ref), 1 - zh


def own_kernel(square_ref, near_ref, second_ref, third_ref, got1_ref, out_ref, got1, square, buf, sems, load_sems):
    load = pltpu.make_async_copy(got1_ref, got1, load_sems.at[0])
    load.start()
    _, g, zh = place()
    copies = []
    for at, (d, mine) in enumerate(((2, second_ref[...]), (3, third_ref[...]), (1, near_ref[...]))):
        w = later(g, d)
        if d == 1:
            copies += put(out_ref, buf, mine, d, w, 0, g, sems, at)
        else:
            turned = -dot(thrice(flip_matrix(1 - w)), thirds(mine))
            copies += put(out_ref, buf, jnp.where(zh == 1, turned, mine), d, w, zh, g, sems, at)
    row, col = iotas(256, G)
    i, j = row >> 4, row & 15
    oi, oj, xi, xj = i >> 3, j >> 3, i & 7, j & 7
    gap = (xj - xi) & 7
    up = 64 + oi * 32 + (gap - 1) * 8 + xi
    down = 64 + oi * 32 + (7 - gap) * 8 + xj
    same = oi == oj
    plus = jnp.where(same, jnp.where((gap >= 1) & (gap <= 4), up, -1), jnp.where(oi < oj, xi * 8 + xj, -1))
    minus = jnp.where(same, jnp.where(gap >= 5, down, -1), jnp.where(oi > oj, xj * 8 + xi, -1))
    pick = (col == plus).astype(jnp.float32) - (col == minus).astype(jnp.float32)
    square[...] = dot(thrice(pick.astype(jnp.bfloat16)), thirds(square_ref[...])).reshape(square.shape)
    copy = pltpu.make_async_copy(square, slab(out_ref, g), load_sems.at[1])
    copy.start()
    copies.append(copy)
    load.wait()
    w = later(g, 1)
    value, turned = returned(got1, 1, w, zh)
    copies += put(out_ref, buf, value, 1, w, turned, g, sems, 3)
    for copy in copies:
        copy.wait()


def back_kernel(d, got_ref, _, out_ref, got, buf, sems, load_sems):
    fetch([(got_ref, got)], load_sems)
    _, g, zh = place()
    w = later(g, d)
    value, turned = returned(got, d, w, zh)
    for copy in put(out_ref, buf, value, d, w, turned, g, sems, 0):
        copy.wait()


def call(kernel, name, outs, args, in_specs, out_specs, scratch=(), aliases={}, room=12):
    return pl.pallas_call(
        kernel,
        out_shape=outs,
        in_specs=in_specs,
        out_specs=out_specs,
        scratch_shapes=scratch,
        input_output_aliases=aliases,
        compiler_params=pltpu.CompilerParams(vmem_limit_bytes=room * MIB),
        cost_estimate=pl.CostEstimate(flops=0, bytes_accessed=0, transcendentals=0),
        name=name,
    )(*args)


def plain(rows, width):
    return jax.ShapeDtypeStruct((rows, width), jnp.float32)


def coded(rows, width):
    return jax.ShapeDtypeStruct((rows + PAD, width), jnp.int16)


def partials(name, groups, offsets, todo, rows, integrals, token, sides, after=None):
    width = integrals.shape[0]
    outs = [coded(G, width) if as_code else plain(G, width) for _, as_code in offsets for _ in range(rows // G)]
    if groups:
        outs.append(jax.ShapeDtypeStruct((rows, 2 * width), jnp.bfloat16))
    args = (todo, *sides, integrals, token)
    specs = [IN_SMEM] + [IN_VMEM] * len(sides) + [IN_HBM, IN_SMEM]
    if after is not None:
        args, specs = (*args, after), [*specs, ANY]
    return call(
        functools.partial(partial_kernel, groups, offsets, after is not None),
        name,
        outs + [TOKEN],
        args,
        specs,
        [IN_VMEM] * len(outs) + [IN_SMEM],
        [
            pltpu.VMEM((len(offsets), 144, RUN, RUN), jnp.bfloat16),
            pltpu.VMEM((len(offsets), rows, width + RUN), jnp.float32),
            pltpu.SemaphoreType.DMA((len(offsets),)),
        ],
        room=50,
    )


def per_device(amplitudes, integrals, pair_irrep, pair_energy, occ_energy):
    i_local, nocc, width = amplitudes.shape
    labels = pair_irrep.reshape(-1, RUN)[:, 0]
    energy = pair_energy.reshape(1, width)
    occ = jnp.broadcast_to(occ_energy[:, None], (nocc, RUN))

    def split(name, go, stay, own, token):
        slabs = len({*go, *stay}) + own
        outs = [jax.ShapeDtypeStruct((G, width), jnp.bfloat16)] * (len(go) + len(stay))
        if own:
            outs.append(jax.ShapeDtypeStruct((256, width), jnp.bfloat16))
        return call(
            functools.partial(split_kernel, go, stay, own),
            name,
            outs,
            (amplitudes, token),
            [IN_HBM, IN_SMEM],
            [IN_VMEM] * len(outs),
            [pltpu.VMEM((slabs, 16, 16, width), jnp.bfloat16), pltpu.SemaphoreType.DMA((slabs,))],
        )

    go2, go3, go1 = split("give", (2, 3, 1), (), False, jnp.zeros((8,), jnp.int32))
    got3 = send(go3, lambda b, o: (b, o ^ 3))
    got2 = send(go2, lambda b, o: (b, o ^ 2))
    got1 = send(go1, lambda b, o: (b, o ^ 1))
    (todo,) = call(
        plan_kernel,
        "plan",
        [jax.ShapeDtypeStruct((8 + 3 * SLOTS,), jnp.int32)],
        (labels,),
        [IN_SMEM],
        [IN_SMEM],
        [pltpu.SMEM((16,), jnp.int32)],
    )
    stay1, stay2, stay3, own = split("keep", (), (1, 2, 3), True, todo)

    square1, near1, square2, near2, near_rows, token = partials(
        "near", (0, 1), ((1, 1), (2, 1)), todo, 2 * G, integrals, todo, (own, stay1, got1)
    )
    near1 = send(near1, lambda b, o: (b + 1, o))
    near2 = send(near2, lambda b, o: (b + 2, o))
    square1 = send(send(square1, lambda b, o: (b, o ^ 2)), lambda b, o: (b ^ 1, o ^ 2))
    far = {}
    for d, stay, got in ((2, stay2, got2), (3, stay3, got3)):
        far1, rows, token = partials("far%d" % d, (d,), ((1, 1),), todo, G, integrals, token, (stay, got))
        far[d] = send(far1, lambda b, o, d=d: (b ^ 1, o ^ d)), rows
    base = {}
    for d in (2, 3):
        far2, far0, token = partials(
            "rest%d" % d, (), ((2, 0), (0, 0)), todo, G, integrals, token, (far[d][1],), None
        )
        base[d] = far0, far2
    square0, near0, token = partials("near0", (), ((0, 0),), todo, 2 * G, integrals, token, (near_rows,))

    onward = {}
    for d in (2, 3):
        far1, _ = far[d]
        (far2,) = call(
            functools.partial(merge_kernel, False),
            "merge%d" % d,
            [coded(G, width)],
            (base[d][1], far1),
            [IN_VMEM, ANY],
            [IN_VMEM],
            [pltpu.VMEM((G + PAD, width), jnp.int16), pltpu.SemaphoreType.DMA((1,))],
        )
        onward[d] = send(far2, lambda b, o: (b + 2, o))

    (square2,) = call(
        functools.partial(merge_kernel, True),
        "merge0",
        [coded(G, width)],
        (square2, square1),
        [IN_VMEM, ANY],
        [IN_VMEM],
        [pltpu.VMEM((G + PAD, width), jnp.int16), pltpu.SemaphoreType.DMA((1,))],
    )
    square2 = send(square2, lambda b, o: (b + 2, o))

    def finish(d, mine, one, two, *after):
        return call(
            functools.partial(finish_kernel, d),
            "finish%d" % d,
            [plain(G, width)] + [coded(G, width)] * (d > 0),
            (mine, one, two, energy, occ, *after),
            [IN_VMEM, ANY, ANY, IN_VMEM, IN_VMEM] + [ANY] * len(after),
            [IN_VMEM] * (1 + (d > 0)),
            [
                pltpu.VMEM((G + PAD, width), jnp.int16),
                pltpu.VMEM((G + PAD, width), jnp.int16),
                pltpu.SemaphoreType.DMA((2,)),
            ],
        )

    done, back = {}, {}
    for d in (2, 3):
        done[d], code = finish(d, base[d][0], far[d][0], onward[d])
        back[d] = send(code, lambda b, o, d=d: (b, o ^ d))
    (square,) = finish(0, square0, square1, square2)
    near, code = finish(1, near0, near1, near2, near0)
    back1 = send(code, lambda b, o: (b, o ^ 1))

    out = jax.ShapeDtypeStruct((i_local, nocc, width), jnp.float32)
    landed = pltpu.VMEM((G + PAD, width), jnp.int16)
    (whole,) = call(
        own_kernel,
        "own",
        [out],
        (square, near, done[2], done[3], back1),
        [IN_VMEM, IN_VMEM, IN_VMEM, IN_VMEM, ANY],
        [ANY],
        [
            landed,
            pltpu.VMEM((16, 16, width), jnp.float32),
            pltpu.VMEM((4, 2, OCT, OCT, width), jnp.float32),
            pltpu.SemaphoreType.DMA((4, 2)),
            pltpu.SemaphoreType.DMA((2,)),
        ],
        room=24,
    )
    for d in (2, 3):
        (whole,) = call(
            functools.partial(back_kernel, d),
            "back%d" % d,
            [out],
            (back[d], whole),
            [ANY, ANY],
            [ANY],
            [
                landed,
                pltpu.VMEM((1, 2, OCT, OCT, width), jnp.float32),
                pltpu.SemaphoreType.DMA((1, 2)),
                pltpu.SemaphoreType.DMA((1,)),
            ],
                aliases={1: 0},
        )
    return whole


def solution(mesh):
    placed = (P("occ", None, "blk"), P("blk", None), P(), P("blk"), P())
    return jax.shard_map(
        per_device, mesh=mesh, in_specs=placed, out_specs=P("occ", None, "blk"), check_vma=False
    )
```

```python
import functools

import jax
import jax.numpy as jnp
from jax import lax
from jax.experimental import pallas as pl
from jax.experimental.pallas import tpu as pltpu
from jax.sharding import PartitionSpec as P

BOTH = ("blk", "occ")
BLOCKS = 32
RUN = 128
OCT = 8
G = 128
PAD = 8
LEVELS = 32000.0
STEPS = 256.0
MANY = 8
LABELS = 8
ORDER = (0, 2, 3)
SLOTS = 160
MIB = 1024 * 1024
ANY = pl.BlockSpec(memory_space=pl.ANY)
IN_VMEM = pl.BlockSpec(memory_space=pltpu.VMEM)
IN_HBM = pl.BlockSpec(memory_space=pltpu.HBM)
IN_SMEM = pl.BlockSpec(memory_space=pltpu.SMEM)
TOKEN = jax.ShapeDtypeStruct((8,), jnp.int32)


def routes(where):
    pairs = []
    for blk in range(BLOCKS):
        for occ in range(4):
            to_blk, to_occ = where(blk, occ)
            pairs.append((blk * 4 + occ, (to_blk % BLOCKS) * 4 + to_occ))
    return pairs


def send(value, where):
    return lax.ppermute(value, BOTH, routes(where))


def place():
    k = lax.axis_index("blk")
    return k, lax.axis_index("occ"), lax.rem(k, 2)


def later(g, d):
    return lax.rem(g, 2) if d == 1 else lax.div(g, 2)


def side(g, zh, d):
    return later(g, d) if d == 1 else lax.rem(later(g, d) + zh, 2)


def apart(g, d):
    low, high = lax.rem(g, 2), lax.div(g, 2)
    low = 1 - low if d & 1 else low
    high = 1 - high if d & 2 else high
    return high * 2 + low


def encode(value, out_ref):
    rows = value.shape[0]
    most = jnp.max(jnp.abs(value), axis=0, keepdims=True)
    code = jnp.ceil(jnp.log2(jnp.maximum(most, 2.0**-120)) * STEPS)
    up = jnp.exp2(code * (-1.0 / STEPS)) * LEVELS
    coded = jnp.clip(jnp.round(value * up), -32767.0, 32767.0)
    out_ref[:rows, :] = coded.astype(jnp.int32).astype(jnp.int16)
    scale = jnp.broadcast_to(code.astype(jnp.int32), (PAD, value.shape[1]))
    out_ref[rows:, :] = scale.astype(jnp.int16)


def scales(ref):
    code = ref[ref.shape[0] - PAD :, :].astype(jnp.int32).astype(jnp.float32)[:1]
    return jnp.exp2(code * (1.0 / STEPS)) * (1.0 / LEVELS)


def codes(ref):
    return ref[: ref.shape[0] - PAD, :].astype(jnp.int32)


def decode(ref):
    return codes(ref).astype(jnp.float32) * scales(ref)


def iotas(rows, cols):
    return (
        lax.broadcasted_iota(jnp.int32, (rows, cols), 0),
        lax.broadcasted_iota(jnp.int32, (rows, cols), 1),
    )


def ones_at(where):
    return where.astype(jnp.float32).astype(jnp.bfloat16)


def flip_matrix(octet_flip):
    row, col = iotas(G, G)
    a, x, y = row >> 6, (row >> 3) & 7, row & 7
    return ones_at(col == (((a ^ octet_flip) << 6) | (y << 3) | x))


def own_pairs(cols):
    row, col = iotas(G, cols)
    q = row - 64
    octet, d, x = q >> 5, ((q >> 3) & 3) + 1, q & 7
    low = row < 64
    i = jnp.where(low, row >> 3, octet * 8 + x)
    j = jnp.where(low, 8 + (row & 7), octet * 8 + ((x + d) & 7))
    return i, j, col


def dot(a, b):
    return jnp.dot(a, b, preferred_element_type=jnp.float32)


def thirds(value):
    high = value.astype(jnp.bfloat16)
    rest = value - high.astype(jnp.float32)
    middle = rest.astype(jnp.bfloat16)
    low = (rest - middle.astype(jnp.float32)).astype(jnp.bfloat16)
    return jnp.concatenate([high, middle, low], axis=0)


def thrice(matrix):
    return jnp.concatenate([matrix, matrix, matrix], axis=1)


def slab(t_ref, group):
    return t_ref.at[:, pl.ds(pl.multiple_of(group * 16, 16), 16), :]


def half(both, s):
    parts = []
    for a in range(2):
        for x in range(OCT):
            one = both[a * OCT + x].astype(jnp.float32)
            parts.append(jnp.where((a ^ s) == 0, one[:OCT], one[OCT:]))
    return jnp.concatenate(parts, axis=0).astype(jnp.bfloat16)


def split_kernel(go, stay, own, t_ref, _, *refs):
    outs, (buf, sems) = refs[:-2], refs[-2:]
    _, g, zh = place()
    ds = sorted({*go, *stay}, reverse=True) + [0] * own
    loads = [pltpu.make_async_copy(slab(t_ref, apart(g, d) if d else g), buf.at[at], sems.at[at]) for at, d in enumerate(ds)]
    for load in loads:
        load.start()
    for load in loads:
        load.wait()
    for at, d in enumerate(go):
        outs[at][...] = half(buf[ds.index(d)], 1 - side(g, zh, d))
    for at, d in enumerate(stay):
        outs[len(go) + at][...] = half(buf[ds.index(d)], side(g, zh, d))
    if own:
        outs[-1][...] = buf[len(ds) - 1].reshape(256, buf.shape[3])


def plan_kernel(lab, todo, begins):
    k, _, _ = place()
    runs = lab.shape[0] // BLOCKS
    rows = [lab[k * runs + r] for r in range(runs)]
    for label in range(LABELS + 1):
        begins[label] = sum((row < label).astype(jnp.int32) for row in rows)
    for s in range(3):
        block = lax.rem(k + s, BLOCKS)
        base = 8 + s * SLOTS

        def column(c, count, block=block, base=base):
            label = lab[block * runs + c]

            def one(r, count):
                todo[base + count] = c * 256 + r * 16 + c
                return count + 1

            return lax.fori_loop(begins[label], begins[label + 1], one, count)

        count = lax.fori_loop(0, runs, column, jnp.int32(0))
        todo[s] = count

        def fill(at, carry, base=base, count=count):
            todo[base + at] = runs * 256 + lax.rem(todo[base + count - 1], 256)
            return carry

        lax.fori_loop(count, lax.div(count + MANY - 1, MANY) * MANY, fill, 0)


def partial_kernel(groups, offsets, after, todo, *refs):
    n = len(groups)
    if n:
        sides = []
        for d in groups:
            sides.append(refs[: 1 + (d > 0)])
            refs = refs[1 + (d > 0) :]
    else:
        lhs, *refs = refs
    v_ref, _, *refs = refs
    if after:
        _, *refs = refs
    acc, parts = refs[-2], refs[-2].shape[1] // G
    outs, refs = refs[: len(offsets) * parts], refs[len(offsets) * parts :]
    if n:
        lhs, *refs = refs
    token, vbuf, acc, sems = refs
    width = v_ref.shape[0]
    runs = width // RUN
    k, g, zh = place()
    token[0] = k

    def tile(s, entry):
        r, c = lax.rem(lax.div(entry, 16), 16), lax.rem(entry, 16)
        return v_ref.at[
            pl.ds(pl.multiple_of(r * RUN, RUN), RUN), pl.ds(pl.multiple_of(s * width + c * RUN, RUN), RUN)
        ]

    for at, (s, _) in enumerate(offsets):

        def begin(e, carry, at=at, s=s):
            source = tile(s, todo[8 + s * SLOTS + e])
            pltpu.make_async_copy(source, vbuf.at[at, e], sems.at[at]).start()
            return carry

        lax.fori_loop(0, todo[s], begin, 0)

    acc[...] = jnp.zeros_like(acc)
    for at, d in enumerate(groups):
        if d:
            s = side(g, zh, d)
            x, y = sides[at][0][...], sides[at][1][...]
            if d >= 2:
                x, y = jnp.where(zh == 1, y, x), jnp.where(zh == 1, x, y)
            y = -dot(flip_matrix(s), y)
        else:
            own = sides[at][0][...]
            i, j, col = own_pairs(256)
            x = dot(ones_at(col == i * 16 + j), own).astype(jnp.bfloat16)
            y = -dot(ones_at(col == j * 16 + i), own)
        y = y.astype(jnp.bfloat16)
        for r in range(runs):
            lhs[at * G : (at + 1) * G, 2 * r * RUN : (2 * r + 1) * RUN] = x[:, r * RUN : (r + 1) * RUN]
            lhs[at * G : (at + 1) * G, (2 * r + 1) * RUN : (2 * r + 2) * RUN] = y[:, r * RUN : (r + 1) * RUN]

    for at, (s, coded) in enumerate(offsets):

        def arrived(e, carry, at=at, s=s):
            pltpu.make_async_copy(tile(s, 0), vbuf.at[at, e], sems.at[at]).wait()
            return carry

        lax.fori_loop(0, todo[s], arrived, 0)

        def several(step, carry, at=at, s=s):
            products = []
            for u in range(MANY):
                e = step * MANY + u
                entry = todo[8 + s * SLOTS + e]
                c, r = lax.div(entry, 256), lax.rem(lax.div(entry, 16), 16)
                right = vbuf[at, jnp.minimum(e, todo[s] - 1)]
                left = lhs[:, pl.ds(pl.multiple_of(r * 2 * RUN, 2 * RUN), 2 * RUN)]
                products.append((c, dot(left, jnp.concatenate([right, right], axis=0))))
            for c, value in products:
                acc[at, :, pl.ds(pl.multiple_of(c * RUN, RUN), RUN)] += value
            return carry

        lax.fori_loop(0, lax.div(todo[s] + MANY - 1, MANY), several, 0)
        for part in range(parts):
            value = acc[at, part * G : (part + 1) * G, :width]
            if coded:
                encode(value, outs[at * parts + part])
            else:
                outs[at * parts + part][...] = value


def fetch(pairs, sems):
    copies = [pltpu.make_async_copy(a, b, sems.at[at]) for at, (a, b) in enumerate(pairs)]
    for copy in copies:
        copy.start()
    for copy in copies:
        copy.wait()


def merge_kernel(plus, mine_ref, got_ref, out_ref, buf, sems):
    fetch([(got_ref, buf)], sems)
    _, _, zh = place()
    mine = decode(mine_ref) if plus else mine_ref[...]
    encode(mine + jnp.where(zh == 0, decode(buf), 0.0), out_ref)


def finished(d, mine, one, two, energy, occ):
    _, g, zh = place()
    if d:
        s = side(g, zh, d)
        row, col = iotas(G, 64)
        a, x, y = row >> 6, (row >> 3) & 7, row & 7
        p = apart(g, d)
        first, second = (g, p) if d == 1 else (jnp.where(zh == 1, p, g), jnp.where(zh == 1, g, p))
        i, j = a * OCT + x + first * 16, (a ^ s) * OCT + y + second * 16
    else:
        i, j, col = own_pairs(64)
        i, j = i + g * 16, j + g * 16
    pick = (col == i).astype(jnp.float32) + (col == j).astype(jnp.float32)
    sums = dot(thrice(pick.astype(jnp.bfloat16)), thirds(occ))[:, :1]
    if d != 1:
        one = jnp.where(zh == 1, one, 0.0)
    return (mine + one + two) / (energy - sums)


def finish_kernel(d, mine_ref, one_ref, two_ref, energy_ref, occ_ref, value_ref, code_ref, one, two, sems):
    fetch([(one_ref, one), (two_ref, two)], sems)
    value = finished(d, mine_ref[...], decode(one), decode(two), energy_ref[...], occ_ref[...])
    value_ref[...] = value
    encode(value, code_ref)


def put(out_ref, buf, value, d, w, turned, g, sems, at):
    p = apart(g, d)
    copies = []
    buf[at] = value.reshape(2, OCT, OCT, value.shape[1])
    for a in range(2):
        o = p * 2 + lax.rem(a + w + turned, 2)
        copy = pltpu.make_async_copy(
            buf.at[at, a],
            out_ref.at[a * OCT : (a + 1) * OCT, pl.ds(pl.multiple_of(o * OCT, OCT), OCT), :],
            sems.at[at, a],
        )
        copy.start()
        copies.append(copy)
    return copies


def returned(ref, d, w, zh):
    code = codes(ref)
    pieces = jnp.concatenate(
        [(code >> 8).astype(jnp.float32).astype(jnp.bfloat16), (code & 255).astype(jnp.float32).astype(jnp.bfloat16)]
    )
    flip = flip_matrix(1 - w).astype(jnp.float32)
    turned = dot(jnp.concatenate([flip * -256.0, -flip], axis=1).astype(jnp.bfloat16), pieces)
    if d == 1:
        return turned * scales(ref), 1
    return jnp.where(zh == 1, code.astype(jnp.float32), turned) * scales(ref), 1 - zh


def own_kernel(near_ref, second_ref, third_ref, got1_ref, out_ref, got1, buf, sems, load_sems):
    load = pltpu.make_async_copy(got1_ref, got1, load_sems.at[0])
    load.start()
    _, g, zh = place()
    copies = []
    for at, (d, mine) in enumerate(((2, second_ref[...]), (3, third_ref[...]), (1, near_ref[...]))):
        w = later(g, d)
        if d == 1:
            copies += put(out_ref, buf, mine, d, w, 0, g, sems, at)
        else:
            turned = -dot(thrice(flip_matrix(1 - w)), thirds(mine))
            copies += put(out_ref, buf, jnp.where(zh == 1, turned, mine), d, w, zh, g, sems, at)
    load.wait()
    w = later(g, 1)
    value, turned = returned(got1, 1, w, zh)
    copies += put(out_ref, buf, value, 1, w, turned, g, sems, 3)
    for copy in copies:
        copy.wait()


def square_kernel(mine_ref, one_ref, two_ref, energy_ref, occ_ref, _, out_ref, one, two, square, sems):
    fetch([(one_ref, one), (two_ref, two)], sems)
    _, g, _ = place()
    value = finished(0, mine_ref[...], decode(one), decode(two), energy_ref[...], occ_ref[...])
    row, col = iotas(256, G)
    i, j = row >> 4, row & 15
    oi, oj, xi, xj = i >> 3, j >> 3, i & 7, j & 7
    gap = (xj - xi) & 7
    up = 64 + oi * 32 + (gap - 1) * 8 + xi
    down = 64 + oi * 32 + (7 - gap) * 8 + xj
    same = oi == oj
    plus = jnp.where(same, jnp.where((gap >= 1) & (gap <= 4), up, -1), jnp.where(oi < oj, xi * 8 + xj, -1))
    minus = jnp.where(same, jnp.where(gap >= 5, down, -1), jnp.where(oi > oj, xj * 8 + xi, -1))
    pick = (col == plus).astype(jnp.float32) - (col == minus).astype(jnp.float32)
    square[...] = dot(thrice(pick.astype(jnp.bfloat16)), thirds(value)).reshape(square.shape)
    fetch([(square, slab(out_ref, g))], sems)


def back_kernel(d, got_ref, _, out_ref, got, buf, sems, load_sems):
    fetch([(got_ref, got)], load_sems)
    _, g, zh = place()
    w = later(g, d)
    value, turned = returned(got, d, w, zh)
    for copy in put(out_ref, buf, value, d, w, turned, g, sems, 0):
        copy.wait()


def call(kernel, name, outs, args, in_specs, out_specs, scratch=(), aliases={}, room=12):
    return pl.pallas_call(
        kernel,
        out_shape=outs,
        in_specs=in_specs,
        out_specs=out_specs,
        scratch_shapes=scratch,
        input_output_aliases=aliases,
        compiler_params=pltpu.CompilerParams(vmem_limit_bytes=room * MIB),
        cost_estimate=pl.CostEstimate(flops=0, bytes_accessed=0, transcendentals=0),
        name=name,
    )(*args)


def plain(rows, width):
    return jax.ShapeDtypeStruct((rows, width), jnp.float32)


def coded(rows, width):
    return jax.ShapeDtypeStruct((rows + PAD, width), jnp.int16)


def partials(name, groups, offsets, todo, rows, integrals, token, sides, after=None):
    width = integrals.shape[0]
    outs = [coded(G, width) if as_code else plain(G, width) for _, as_code in offsets for _ in range(rows // G)]
    if groups:
        outs.append(jax.ShapeDtypeStruct((rows, 2 * width), jnp.bfloat16))
    args = (todo, *sides, integrals, token)
    specs = [IN_SMEM] + [IN_VMEM] * len(sides) + [IN_HBM, IN_SMEM]
    if after is not None:
        args, specs = (*args, after), [*specs, ANY]
    return call(
        functools.partial(partial_kernel, groups, offsets, after is not None),
        name,
        outs + [TOKEN],
        args,
        specs,
        [IN_VMEM] * len(outs) + [IN_SMEM],
        [
            pltpu.VMEM((len(offsets), 144, RUN, RUN), jnp.bfloat16),
            pltpu.VMEM((len(offsets), rows, width + RUN), jnp.float32),
            pltpu.SemaphoreType.DMA((len(offsets),)),
        ],
        room=50,
    )


def per_device(amplitudes, integrals, pair_irrep, pair_energy, occ_energy):
    i_local, nocc, width = amplitudes.shape
    labels = pair_irrep.reshape(-1, RUN)[:, 0]
    energy = pair_energy.reshape(1, width)
    occ = jnp.broadcast_to(occ_energy[:, None], (nocc, RUN))

    def split(name, go, stay, own, token):
        slabs = len({*go, *stay}) + own
        outs = [jax.ShapeDtypeStruct((G, width), jnp.bfloat16)] * (len(go) + len(stay))
        if own:
            outs.append(jax.ShapeDtypeStruct((256, width), jnp.bfloat16))
        return call(
            functools.partial(split_kernel, go, stay, own),
            name,
            outs,
            (amplitudes, token),
            [IN_HBM, IN_SMEM],
            [IN_VMEM] * len(outs),
            [pltpu.VMEM((slabs, 16, 16, width), jnp.bfloat16), pltpu.SemaphoreType.DMA((slabs,))],
        )

    go2, go3, go1 = split("give", (2, 3, 1), (), False, jnp.zeros((8,), jnp.int32))
    got3 = send(go3, lambda b, o: (b, o ^ 3))
    got2 = send(go2, lambda b, o: (b, o ^ 2))
    got1 = send(go1, lambda b, o: (b, o ^ 1))
    (todo,) = call(
        plan_kernel,
        "plan",
        [jax.ShapeDtypeStruct((8 + 3 * SLOTS,), jnp.int32)],
        (labels,),
        [IN_SMEM],
        [IN_SMEM],
        [pltpu.SMEM((16,), jnp.int32)],
    )
    stay1, stay2, stay3, own = split("keep", (), (1, 2, 3), True, jnp.zeros((8,), jnp.int32))

    square1, near1, square2, near2, near_rows, token = partials(
        "near", (0, 1), ((1, 1), (2, 1)), todo, 2 * G, integrals, todo, (own, stay1, got1)
    )
    near1 = send(near1, lambda b, o: (b + 1, o))
    near2 = send(near2, lambda b, o: (b + 2, o))
    square1 = send(send(square1, lambda b, o: (b, o ^ 2)), lambda b, o: (b ^ 1, o ^ 2))
    far = {}
    for d, stay, got in ((2, stay2, got2), (3, stay3, got3)):
        far1, rows, token = partials("far%d" % d, (d,), ((1, 1),), todo, G, integrals, token, (stay, got))
        far[d] = send(far1, lambda b, o, d=d: (b ^ 1, o ^ d)), rows
    base = {}
    for d in (2, 3):
        far2, far0, token = partials(
            "rest%d" % d, (), ((2, 0), (0, 0)), todo, G, integrals, token, (far[d][1],), None
        )
        base[d] = far0, far2
    square0, near0, token = partials("near0", (), ((0, 0),), todo, 2 * G, integrals, token, (near_rows,))

    onward = {}
    for d in (2, 3):
        far1, _ = far[d]
        (far2,) = call(
            functools.partial(merge_kernel, False),
            "merge%d" % d,
            [coded(G, width)],
            (base[d][1], far1),
            [IN_VMEM, ANY],
            [IN_VMEM],
            [pltpu.VMEM((G + PAD, width), jnp.int16), pltpu.SemaphoreType.DMA((1,))],
        )
        onward[d] = send(far2, lambda b, o: (b + 2, o))

    (square2,) = call(
        functools.partial(merge_kernel, True),
        "merge0",
        [coded(G, width)],
        (square2, square1),
        [IN_VMEM, ANY],
        [IN_VMEM],
        [pltpu.VMEM((G + PAD, width), jnp.int16), pltpu.SemaphoreType.DMA((1,))],
    )
    square2 = send(square2, lambda b, o: (b + 2, o))

    landed = pltpu.VMEM((G + PAD, width), jnp.int16)

    def finish(d, mine, one, two):
        return call(
            functools.partial(finish_kernel, d),
            "finish%d" % d,
            [plain(G, width), coded(G, width)],
            (mine, one, two, energy, occ),
            [IN_VMEM, ANY, ANY, IN_VMEM, IN_VMEM],
            [IN_VMEM] * 2,
            [landed, landed, pltpu.SemaphoreType.DMA((2,))],
        )

    done, back = {}, {}
    for d in (2, 3):
        done[d], code = finish(d, base[d][0], far[d][0], onward[d])
        back[d] = send(code, lambda b, o, d=d: (b, o ^ d))
    near, code = finish(1, near0, near1, near2)
    back1 = send(code, lambda b, o: (b, o ^ 1))

    out = jax.ShapeDtypeStruct((i_local, nocc, width), jnp.float32)
    (whole,) = call(
        own_kernel,
        "own",
        [out],
        (near, done[2], done[3], back1),
        [IN_VMEM, IN_VMEM, IN_VMEM, ANY],
        [ANY],
        [
            landed,
            pltpu.VMEM((4, 2, OCT, OCT, width), jnp.float32),
            pltpu.SemaphoreType.DMA((4, 2)),
            pltpu.SemaphoreType.DMA((1,)),
        ],
        room=24,
    )
    for d in ORDER:
        if d == 0:
            (whole,) = call(
                square_kernel,
                "square",
                [out],
                (square0, square1, square2, energy, occ, whole),
                [IN_VMEM, ANY, ANY, IN_VMEM, IN_VMEM, ANY],
                [ANY],
                [landed, landed, pltpu.VMEM((16, 16, width), jnp.float32), pltpu.SemaphoreType.DMA((2,))],
                aliases={5: 0},
            )
            continue
        (whole,) = call(
            functools.partial(back_kernel, d),
            "back%d" % d,
            [out],
            (back[d], whole),
            [ANY, ANY],
            [ANY],
            [
                landed,
                pltpu.VMEM((1, 2, OCT, OCT, width), jnp.float32),
                pltpu.SemaphoreType.DMA((1, 2)),
                pltpu.SemaphoreType.DMA((1,)),
            ],
            aliases={1: 0},
        )
    return whole


def solution(mesh):
    placed = (P("occ", None, "blk"), P("blk", None), P(), P("blk"), P())
    return jax.shard_map(
        per_device, mesh=mesh, in_specs=placed, out_specs=P("occ", None, "blk"), check_vma=False
    )
```

```python
import functools

import jax
import jax.numpy as jnp
from jax import lax
from jax.experimental import pallas as pl
from jax.experimental.pallas import tpu as pltpu
from jax.sharding import PartitionSpec as P

BOTH = ("blk", "occ")
BLOCKS = 32
RUN = 128
OCT = 8
G = 128
PAD = 8
LEVELS = 32000.0
STEPS = 256.0
MANY = 4
LABELS = 8
ORDER = (0, 2, 3)
SLOTS = 160
MIB = 1024 * 1024
ANY = pl.BlockSpec(memory_space=pl.ANY)
IN_VMEM = pl.BlockSpec(memory_space=pltpu.VMEM)
IN_HBM = pl.BlockSpec(memory_space=pltpu.HBM)
IN_SMEM = pl.BlockSpec(memory_space=pltpu.SMEM)
TOKEN = jax.ShapeDtypeStruct((8,), jnp.int32)


def routes(where):
    pairs = []
    for blk in range(BLOCKS):
        for occ in range(4):
            to_blk, to_occ = where(blk, occ)
            pairs.append((blk * 4 + occ, (to_blk % BLOCKS) * 4 + to_occ))
    return pairs


def send(value, where):
    return lax.ppermute(value, BOTH, routes(where))


def place():
    k = lax.axis_index("blk")
    return k, lax.axis_index("occ"), lax.rem(k, 2)


def later(g, d):
    return lax.rem(g, 2) if d == 1 else lax.div(g, 2)


def side(g, zh, d):
    return later(g, d) if d == 1 else lax.rem(later(g, d) + zh, 2)


def apart(g, d):
    low, high = lax.rem(g, 2), lax.div(g, 2)
    low = 1 - low if d & 1 else low
    high = 1 - high if d & 2 else high
    return high * 2 + low


def encode(value, out_ref):
    rows = value.shape[0]
    most = jnp.max(jnp.abs(value), axis=0, keepdims=True)
    code = jnp.ceil(jnp.log2(jnp.maximum(most, 2.0**-120)) * STEPS)
    up = jnp.exp2(code * (-1.0 / STEPS)) * LEVELS
    coded = jnp.clip(jnp.round(value * up), -32767.0, 32767.0)
    out_ref[:rows, :] = coded.astype(jnp.int32).astype(jnp.int16)
    scale = jnp.broadcast_to(code.astype(jnp.int32), (PAD, value.shape[1]))
    out_ref[rows:, :] = scale.astype(jnp.int16)


def scales(ref):
    code = ref[ref.shape[0] - PAD :, :].astype(jnp.int32).astype(jnp.float32)[:1]
    return jnp.exp2(code * (1.0 / STEPS)) * (1.0 / LEVELS)


def codes(ref):
    return ref[: ref.shape[0] - PAD, :].astype(jnp.int32)


def decode(ref):
    return codes(ref).astype(jnp.float32) * scales(ref)


def iotas(rows, cols):
    return (
        lax.broadcasted_iota(jnp.int32, (rows, cols), 0),
        lax.broadcasted_iota(jnp.int32, (rows, cols), 1),
    )


def ones_at(where):
    return where.astype(jnp.float32).astype(jnp.bfloat16)


def flip_matrix(octet_flip):
    row, col = iotas(G, G)
    a, x, y = row >> 6, (row >> 3) & 7, row & 7
    return ones_at(col == (((a ^ octet_flip) << 6) | (y << 3) | x))


def own_pairs(cols):
    row, col = iotas(G, cols)
    q = row - 64
    octet, d, x = q >> 5, ((q >> 3) & 3) + 1, q & 7
    low = row < 64
    i = jnp.where(low, row >> 3, octet * 8 + x)
    j = jnp.where(low, 8 + (row & 7), octet * 8 + ((x + d) & 7))
    return i, j, col


def dot(a, b):
    return jnp.dot(a, b, preferred_element_type=jnp.float32)


def thirds(value):
    high = value.astype(jnp.bfloat16)
    rest = value - high.astype(jnp.float32)
    middle = rest.astype(jnp.bfloat16)
    low = (rest - middle.astype(jnp.float32)).astype(jnp.bfloat16)
    return jnp.concatenate([high, middle, low], axis=0)


def thrice(matrix):
    return jnp.concatenate([matrix, matrix, matrix], axis=1)


def slab(t_ref, group):
    return t_ref.at[:, pl.ds(pl.multiple_of(group * 16, 16), 16), :]


def half(both, s):
    parts = []
    for a in range(2):
        for x in range(OCT):
            one = both[a * OCT + x].astype(jnp.float32)
            parts.append(jnp.where((a ^ s) == 0, one[:OCT], one[OCT:]))
    return jnp.concatenate(parts, axis=0).astype(jnp.bfloat16)


def split_kernel(go, stay, own, t_ref, _, *refs):
    outs, (buf, sems) = refs[:-2], refs[-2:]
    _, g, zh = place()
    ds = sorted({*go, *stay}, reverse=True) + [0] * own
    loads = [pltpu.make_async_copy(slab(t_ref, apart(g, d) if d else g), buf.at[at], sems.at[at]) for at, d in enumerate(ds)]
    for load in loads:
        load.start()
    for load in loads:
        load.wait()
    for at, d in enumerate(go):
        outs[at][...] = half(buf[ds.index(d)], 1 - side(g, zh, d))
    for at, d in enumerate(stay):
        outs[len(go) + at][...] = half(buf[ds.index(d)], side(g, zh, d))
    if own:
        outs[-1][...] = buf[len(ds) - 1].reshape(256, buf.shape[3])


def plan_kernel(lab, todo, begins):
    k, _, _ = place()
    runs = lab.shape[0] // BLOCKS
    rows = [lab[k * runs + r] for r in range(runs)]
    for label in range(LABELS + 1):
        begins[label] = sum((row < label).astype(jnp.int32) for row in rows)
    for s in range(3):
        block = lax.rem(k + s, BLOCKS)
        base = 8 + s * SLOTS

        def column(c, count, block=block, base=base):
            label = lab[block * runs + c]

            def one(r, count):
                todo[base + count] = c * 256 + r * 16 + c
                return count + 1

            return lax.fori_loop(begins[label], begins[label + 1], one, count)

        count = lax.fori_loop(0, runs, column, jnp.int32(0))
        todo[s] = count

        def fill(at, carry, base=base, count=count):
            todo[base + at] = runs * 256 + lax.rem(todo[base + count - 1], 256)
            return carry

        lax.fori_loop(count, lax.div(count + MANY - 1, MANY) * MANY, fill, 0)


def partial_kernel(groups, offsets, after, todo, *refs):
    n = len(groups)
    if n:
        sides = []
        for d in groups:
            sides.append(refs[: 1 + (d > 0)])
            refs = refs[1 + (d > 0) :]
    else:
        lhs, *refs = refs
    v_ref, _, *refs = refs
    if after:
        _, *refs = refs
    acc, parts = refs[-2], refs[-2].shape[1] // G
    outs, refs = refs[: len(offsets) * parts], refs[len(offsets) * parts :]
    if n:
        lhs, *refs = refs
    token, vbuf, acc, sems = refs
    width = v_ref.shape[0]
    runs = width // RUN
    k, g, zh = place()
    token[0] = k

    def tile(s, entry):
        r, c = lax.rem(lax.div(entry, 16), 16), lax.rem(entry, 16)
        return v_ref.at[
            pl.ds(pl.multiple_of(r * RUN, RUN), RUN), pl.ds(pl.multiple_of(s * width + c * RUN, RUN), RUN)
        ]

    for at, (s, _) in enumerate(offsets):

        def begin(e, carry, at=at, s=s):
            source = tile(s, todo[8 + s * SLOTS + e])
            pltpu.make_async_copy(source, vbuf.at[at, e], sems.at[at]).start()
            return carry

        lax.fori_loop(0, todo[s], begin, 0)

    acc[...] = jnp.zeros_like(acc)
    for at, d in enumerate(groups):
        if d:
            s = side(g, zh, d)
            x, y = sides[at][0][...], sides[at][1][...]
            if d >= 2:
                x, y = jnp.where(zh == 1, y, x), jnp.where(zh == 1, x, y)
            y = -dot(flip_matrix(s), y)
        else:
            own = sides[at][0][...]
            i, j, col = own_pairs(256)
            x = dot(ones_at(col == i * 16 + j), own).astype(jnp.bfloat16)
            y = -dot(ones_at(col == j * 16 + i), own)
        y = y.astype(jnp.bfloat16)
        for r in range(runs):
            lhs[at * G : (at + 1) * G, 2 * r * RUN : (2 * r + 1) * RUN] = x[:, r * RUN : (r + 1) * RUN]
            lhs[at * G : (at + 1) * G, (2 * r + 1) * RUN : (2 * r + 2) * RUN] = y[:, r * RUN : (r + 1) * RUN]

    for at, (s, coded) in enumerate(offsets):

        def arrived(e, carry, at=at, s=s):
            pltpu.make_async_copy(tile(s, 0), vbuf.at[at, e], sems.at[at]).wait()
            return carry

        lax.fori_loop(0, todo[s], arrived, 0)

        def several(step, carry, at=at, s=s):
            products = []
            for u in range(MANY):
                e = step * MANY + u
                entry = todo[8 + s * SLOTS + e]
                c, r = lax.div(entry, 256), lax.rem(lax.div(entry, 16), 16)
                right = vbuf[at, jnp.minimum(e, todo[s] - 1)]
                left = lhs[:, pl.ds(pl.multiple_of(r * 2 * RUN, 2 * RUN), 2 * RUN)]
                products.append((c, dot(left, jnp.concatenate([right, right], axis=0))))
            for c, value in products:
                acc[at, :, pl.ds(pl.multiple_of(c * RUN, RUN), RUN)] += value
            return carry

        lax.fori_loop(0, lax.div(todo[s] + MANY - 1, MANY), several, 0)
        for part in range(parts):
            value = acc[at, part * G : (part + 1) * G, :width]
            if coded:
                encode(value, outs[at * parts + part])
            else:
                outs[at * parts + part][...] = value


def fetch(pairs, sems):
    copies = [pltpu.make_async_copy(a, b, sems.at[at]) for at, (a, b) in enumerate(pairs)]
    for copy in copies:
        copy.start()
    for copy in copies:
        copy.wait()


def merge_kernel(plus, mine_ref, got_ref, out_ref, buf, sems):
    fetch([(got_ref, buf)], sems)
    _, _, zh = place()
    mine = decode(mine_ref) if plus else mine_ref[...]
    encode(mine + jnp.where(zh == 0, decode(buf), 0.0), out_ref)


def finished(d, mine, one, two, energy, occ):
    _, g, zh = place()
    if d:
        s = side(g, zh, d)
        row, col = iotas(G, 64)
        a, x, y = row >> 6, (row >> 3) & 7, row & 7
        p = apart(g, d)
        first, second = (g, p) if d == 1 else (jnp.where(zh == 1, p, g), jnp.where(zh == 1, g, p))
        i, j = a * OCT + x + first * 16, (a ^ s) * OCT + y + second * 16
    else:
        i, j, col = own_pairs(64)
        i, j = i + g * 16, j + g * 16
    pick = (col == i).astype(jnp.float32) + (col == j).astype(jnp.float32)
    sums = dot(thrice(pick.astype(jnp.bfloat16)), thirds(occ))[:, :1]
    if d != 1:
        one = jnp.where(zh == 1, one, 0.0)
    return (mine + one + two) / (energy - sums)


def finish_kernel(d, mine_ref, one_ref, two_ref, energy_ref, occ_ref, value_ref, code_ref, one, two, sems):
    fetch([(one_ref, one), (two_ref, two)], sems)
    value = finished(d, mine_ref[...], decode(one), decode(two), energy_ref[...], occ_ref[...])
    value_ref[...] = value
    encode(value, code_ref)


def put(out_ref, buf, value, d, w, turned, g, sems, at):
    p = apart(g, d)
    copies = []
    buf[at] = value.reshape(2, OCT, OCT, value.shape[1])
    for a in range(2):
        o = p * 2 + lax.rem(a + w + turned, 2)
        copy = pltpu.make_async_copy(
            buf.at[at, a],
            out_ref.at[a * OCT : (a + 1) * OCT, pl.ds(pl.multiple_of(o * OCT, OCT), OCT), :],
            sems.at[at, a],
        )
        copy.start()
        copies.append(copy)
    return copies


def returned(ref, d, w, zh):
    code = codes(ref)
    pieces = jnp.concatenate(
        [(code >> 8).astype(jnp.float32).astype(jnp.bfloat16), (code & 255).astype(jnp.float32).astype(jnp.bfloat16)]
    )
    flip = flip_matrix(1 - w).astype(jnp.float32)
    turned = dot(jnp.concatenate([flip * -256.0, -flip], axis=1).astype(jnp.bfloat16), pieces)
    if d == 1:
        return turned * scales(ref), 1
    return jnp.where(zh == 1, code.astype(jnp.float32), turned) * scales(ref), 1 - zh


def own_kernel(near_ref, second_ref, third_ref, got1_ref, out_ref, got1, buf, sems, load_sems):
    load = pltpu.make_async_copy(got1_ref, got1, load_sems.at[0])
    load.start()
    _, g, zh = place()
    copies = []
    for at, (d, mine) in enumerate(((2, second_ref[...]), (3, third_ref[...]), (1, near_ref[...]))):
        w = later(g, d)
        if d == 1:
            copies += put(out_ref, buf, mine, d, w, 0, g, sems, at)
        else:
            turned = -dot(thrice(flip_matrix(1 - w)), thirds(mine))
            copies += put(out_ref, buf, jnp.where(zh == 1, turned, mine), d, w, zh, g, sems, at)
    load.wait()
    w = later(g, 1)
    value, turned = returned(got1, 1, w, zh)
    copies += put(out_ref, buf, value, 1, w, turned, g, sems, 3)
    for copy in copies:
        copy.wait()


def square_kernel(mine_ref, one_ref, two_ref, energy_ref, occ_ref, _, out_ref, one, two, square, sems):
    fetch([(one_ref, one), (two_ref, two)], sems)
    _, g, _ = place()
    value = finished(0, mine_ref[...], decode(one), decode(two), energy_ref[...], occ_ref[...])
    row, col = iotas(256, G)
    i, j = row >> 4, row & 15
    oi, oj, xi, xj = i >> 3, j >> 3, i & 7, j & 7
    gap = (xj - xi) & 7
    up = 64 + oi * 32 + (gap - 1) * 8 + xi
    down = 64 + oi * 32 + (7 - gap) * 8 + xj
    same = oi == oj
    plus = jnp.where(same, jnp.where((gap >= 1) & (gap <= 4), up, -1), jnp.where(oi < oj, xi * 8 + xj, -1))
    minus = jnp.where(same, jnp.where(gap >= 5, down, -1), jnp.where(oi > oj, xj * 8 + xi, -1))
    pick = (col == plus).astype(jnp.float32) - (col == minus).astype(jnp.float32)
    square[...] = dot(thrice(pick.astype(jnp.bfloat16)), thirds(value)).reshape(square.shape)
    fetch([(square, slab(out_ref, g))], sems)


def back_kernel(d, got_ref, _, out_ref, got, buf, sems, load_sems):
    fetch([(got_ref, got)], load_sems)
    _, g, zh = place()
    w = later(g, d)
    value, turned = returned(got, d, w, zh)
    for copy in put(out_ref, buf, value, d, w, turned, g, sems, 0):
        copy.wait()


def call(kernel, name, outs, args, in_specs, out_specs, scratch=(), aliases={}, room=12):
    return pl.pallas_call(
        kernel,
        out_shape=outs,
        in_specs=in_specs,
        out_specs=out_specs,
        scratch_shapes=scratch,
        input_output_aliases=aliases,
        compiler_params=pltpu.CompilerParams(vmem_limit_bytes=room * MIB),
        cost_estimate=pl.CostEstimate(flops=0, bytes_accessed=0, transcendentals=0),
        name=name,
    )(*args)


def plain(rows, width):
    return jax.ShapeDtypeStruct((rows, width), jnp.float32)


def coded(rows, width):
    return jax.ShapeDtypeStruct((rows + PAD, width), jnp.int16)


def partials(name, groups, offsets, todo, rows, integrals, token, sides, after=None):
    width = integrals.shape[0]
    outs = [coded(G, width) if as_code else plain(G, width) for _, as_code in offsets for _ in range(rows // G)]
    if groups:
        outs.append(jax.ShapeDtypeStruct((rows, 2 * width), jnp.bfloat16))
    args = (todo, *sides, integrals, token)
    specs = [IN_SMEM] + [IN_VMEM] * len(sides) + [IN_HBM, IN_SMEM]
    if after is not None:
        args, specs = (*args, after), [*specs, ANY]
    return call(
        functools.partial(partial_kernel, groups, offsets, after is not None),
        name,
        outs + [TOKEN],
        args,
        specs,
        [IN_VMEM] * len(outs) + [IN_SMEM],
        [
            pltpu.VMEM((len(offsets), 144, RUN, RUN), jnp.bfloat16),
            pltpu.VMEM((len(offsets), rows, width + RUN), jnp.float32),
            pltpu.SemaphoreType.DMA((len(offsets),)),
        ],
        room=50,
    )


def per_device(amplitudes, integrals, pair_irrep, pair_energy, occ_energy):
    i_local, nocc, width = amplitudes.shape
    labels = pair_irrep.reshape(-1, RUN)[:, 0]
    energy = pair_energy.reshape(1, width)
    occ = jnp.broadcast_to(occ_energy[:, None], (nocc, RUN))

    def split(name, go, stay, own, token):
        slabs = len({*go, *stay}) + own
        outs = [jax.ShapeDtypeStruct((G, width), jnp.bfloat16)] * (len(go) + len(stay))
        if own:
            outs.append(jax.ShapeDtypeStruct((256, width), jnp.bfloat16))
        return call(
            functools.partial(split_kernel, go, stay, own),
            name,
            outs,
            (amplitudes, token),
            [IN_HBM, IN_SMEM],
            [IN_VMEM] * len(outs),
            [pltpu.VMEM((slabs, 16, 16, width), jnp.bfloat16), pltpu.SemaphoreType.DMA((slabs,))],
        )

    go2, go3, go1 = split("give", (2, 3, 1), (), False, jnp.zeros((8,), jnp.int32))
    got3 = send(go3, lambda b, o: (b, o ^ 3))
    got2 = send(go2, lambda b, o: (b, o ^ 2))
    got1 = send(go1, lambda b, o: (b, o ^ 1))
    (todo,) = call(
        plan_kernel,
        "plan",
        [jax.ShapeDtypeStruct((8 + 3 * SLOTS,), jnp.int32)],
        (labels,),
        [IN_SMEM],
        [IN_SMEM],
        [pltpu.SMEM((16,), jnp.int32)],
    )
    stay1, stay2, stay3, own = split("keep", (), (1, 2, 3), True, jnp.zeros((8,), jnp.int32))

    square1, near1, square2, near2, near_rows, token = partials(
        "near", (0, 1), ((1, 1), (2, 1)), todo, 2 * G, integrals, todo, (own, stay1, got1)
    )
    near1 = send(near1, lambda b, o: (b + 1, o))
    near2 = send(near2, lambda b, o: (b + 2, o))
    square1 = send(send(square1, lambda b, o: (b, o ^ 2)), lambda b, o: (b ^ 1, o ^ 2))
    far = {}
    for d, stay, got in ((2, stay2, got2), (3, stay3, got3)):
        far1, rows, token = partials("far%d" % d, (d,), ((1, 1),), todo, G, integrals, token, (stay, got))
        far[d] = send(far1, lambda b, o, d=d: (b ^ 1, o ^ d)), rows
    base = {}
    for d in (2, 3):
        far2, far0, token = partials(
            "rest%d" % d, (), ((2, 0), (0, 0)), todo, G, integrals, token, (far[d][1],), None
        )
        base[d] = far0, far2
    square0, near0, token = partials("near0", (), ((0, 0),), todo, 2 * G, integrals, token, (near_rows,))

    onward = {}
    for d in (2, 3):
        far1, _ = far[d]
        (far2,) = call(
            functools.partial(merge_kernel, False),
            "merge%d" % d,
            [coded(G, width)],
            (base[d][1], far1),
            [IN_VMEM, ANY],
            [IN_VMEM],
            [pltpu.VMEM((G + PAD, width), jnp.int16), pltpu.SemaphoreType.DMA((1,))],
        )
        onward[d] = send(far2, lambda b, o: (b + 2, o))

    (square2,) = call(
        functools.partial(merge_kernel, True),
        "merge0",
        [coded(G, width)],
        (square2, square1),
        [IN_VMEM, ANY],
        [IN_VMEM],
        [pltpu.VMEM((G + PAD, width), jnp.int16), pltpu.SemaphoreType.DMA((1,))],
    )
    square2 = send(square2, lambda b, o: (b + 2, o))

    landed = pltpu.VMEM((G + PAD, width), jnp.int16)

    def finish(d, mine, one, two):
        return call(
            functools.partial(finish_kernel, d),
            "finish%d" % d,
            [plain(G, width), coded(G, width)],
            (mine, one, two, energy, occ),
            [IN_VMEM, ANY, ANY, IN_VMEM, IN_VMEM],
            [IN_VMEM] * 2,
            [landed, landed, pltpu.SemaphoreType.DMA((2,))],
        )

    done, back = {}, {}
    for d in (2, 3):
        done[d], code = finish(d, base[d][0], far[d][0], onward[d])
        back[d] = send(code, lambda b, o, d=d: (b, o ^ d))
    near, code = finish(1, near0, near1, near2)
    back1 = send(code, lambda b, o: (b, o ^ 1))

    out = jax.ShapeDtypeStruct((i_local, nocc, width), jnp.float32)
    (whole,) = call(
        own_kernel,
        "own",
        [out],
        (near, done[2], done[3], back1),
        [IN_VMEM, IN_VMEM, IN_VMEM, ANY],
        [ANY],
        [
            landed,
            pltpu.VMEM((4, 2, OCT, OCT, width), jnp.float32),
            pltpu.SemaphoreType.DMA((4, 2)),
            pltpu.SemaphoreType.DMA((1,)),
        ],
        room=24,
    )
    for d in ORDER:
        if d == 0:
            (whole,) = call(
                square_kernel,
                "square",
                [out],
                (square0, square1, square2, energy, occ, whole),
                [IN_VMEM, ANY, ANY, IN_VMEM, IN_VMEM, ANY],
                [ANY],
                [landed, landed, pltpu.VMEM((16, 16, width), jnp.float32), pltpu.SemaphoreType.DMA((2,))],
                aliases={5: 0},
            )
            continue
        (whole,) = call(
            functools.partial(back_kernel, d),
            "back%d" % d,
            [out],
            (back[d], whole),
            [ANY, ANY],
            [ANY],
            [
                landed,
                pltpu.VMEM((1, 2, OCT, OCT, width), jnp.float32),
                pltpu.SemaphoreType.DMA((1, 2)),
                pltpu.SemaphoreType.DMA((1,)),
            ],
            aliases={1: 0},
        )
    return whole


def solution(mesh):
    placed = (P("occ", None, "blk"), P("blk", None), P(), P("blk"), P())
    return jax.shard_map(
        per_device, mesh=mesh, in_specs=placed, out_specs=P("occ", None, "blk"), check_vma=False
    )
```
